128 devices in a mesh: slab: 4 (over y_lo, core), pencil: 32 (over x, z, y_hi).
Axes of the slice: x: 4, y: 4 (y_hi: 2, y_lo: 2; y = y_hi * 2 + y_lo), z: 4, core: 2. Of those that a mesh axis runs over, the one named last changes fastest.
Arguments:
- density: float32 [16, 256, 4096], P('slab', 'pencil'), parts along dimension 0, may hold values from 0.5 to 2
- velocity: float32 [2, 16, 256, 4096], P(None, 'slab', 'pencil'), parts along dimension 1, may hold values from -2.5 to 2.5
- pressure: float32 [16, 256, 4096], P('slab', 'pencil'), parts along dimension 0, may hold values from 0.5 to 2
Outputs:
- new_density: float32 [16, 256, 4096], P('slab', 'pencil'), parts along dimension 0
- new_velocity: float32 [2, 16, 256, 4096], P(None, 'slab', 'pencil'), parts along dimension 1
- new_pressure: float32 [16, 256, 4096], P('slab', 'pencil'), parts along dimension 0
The draws below stay inside these ranges and needn't reach their ends.
There are 4 independent parts, one for each index of `slab`. The reference program is written for one: setup_inputs(seed, part) draws one part's arguments, and reference() takes and returns one part's arrays. A program takes and returns all parts, laid end to end along the dimension named above; each array names one. Nothing has to cross between parts.
All inputs are finite; a program needn't handle non-finite values.
Results may differ from the reference program's by a relative error of at most 0.00002.
Values sent between devices are 32-bit elements; how exact they have to be, the bound alone decides.
A program may use at most 64 MiB of HBM per device.

```python
import math
import jax
import jax.numpy as jnp

NX = 4096
PLANES = 4
NEWTON = 4
NY = 256


def level_of(key, extent, pieces, low, largest):
    level, own = 1.0, jax.random.fold_in(key, 6)
    for position, parts in pieces:
        draws = jnp.exp(jax.random.uniform(jax.random.fold_in(own, position), (parts,), jnp.float32, low / len(pieces), largest / len(pieces)))
        level = level * jnp.repeat(draws, extent[position] // parts).reshape([-1 if axis == position else 1 for axis in range(len(extent))])
    return level


def gaussian(stream_key, extent, spread, most, pieces=(), dtype=jnp.bfloat16):
    result = spread * jax.random.normal(stream_key, extent, jnp.float32)
    if pieces:
        result = result * level_of(stream_key, extent, pieces, -0.22, 0.18)
    return jnp.clip(result, -most, most).astype(dtype)


def setup_inputs(seed: int = 0, part: int = 0) -> dict:
    key_list = jax.random.split(jax.random.key(seed), 4)
    own_keys = jax.random.split(jax.random.fold_in(key_list[3], part), 4)
    density = jnp.clip(jnp.exp(math.log(2.0) - 1.3862944 * jax.random.uniform(own_keys[0], (PLANES, NY, NX), jnp.float32) ** level_of(own_keys[0], (PLANES, NY, NX), ((1, 32),), -0.2, 0.2)), 0.5, 2.0)
    velocity = gaussian(own_keys[1], (2, PLANES, NY, NX), 0.5, 2.5, ((2, 32),), jnp.float32)
    pressure = jnp.clip(jnp.exp(math.log(2.0) - 1.3862944 * jax.random.uniform(own_keys[2], (PLANES, NY, NX), jnp.float32) ** level_of(own_keys[2], (PLANES, NY, NX), ((1, 32),), -0.2, 0.2)), 0.5, 2.0)
    return dict(density=density, velocity=velocity, pressure=pressure)


gamma_gas = 1.4

def reconstruct(values, axis):
    nextv = jnp.roll(values, -1, axis)
    prevv = jnp.roll(values, 1, axis)
    next_two = jnp.roll(values, -2, axis)
    face = (7.0 * (values + nextv) - (prevv + next_two)) / 12.0
    face = jnp.clip(face, jnp.minimum(values, nextv), jnp.maximum(values, nextv))
    right_diff = face - values
    left_diff = jnp.roll(face, 1, axis) - values
    left_lim = jnp.clip(left_diff, -2.0 * jnp.abs(right_diff), 2.0 * jnp.abs(right_diff))
    right_lim = jnp.clip(right_diff, -2.0 * jnp.abs(left_diff), 2.0 * jnp.abs(left_diff))
    left_state = values + right_lim
    right_state = jnp.roll(values + left_lim, -1, axis)
    return (left_state, right_state)

def riemann(rho_l, un_l, p_l, rho_r, un_r, p_r):
    c_l = jnp.sqrt(gamma_gas * p_l * rho_l)
    c_r = jnp.sqrt(gamma_gas * p_r * rho_r)
    floor_p = 0.1 * jnp.minimum(p_l, p_r)
    pstar = (c_r * p_l + c_l * p_r + c_l * c_r * (un_l - un_r)) / (c_l + c_r)
    pstar = jnp.maximum(pstar, floor_p)
    for count in range(NEWTON):
        w_l = jnp.sqrt(rho_l * (0.5 * (gamma_gas + 1.0) * pstar + 0.5 * (gamma_gas - 1.0) * p_l))
        w_r = jnp.sqrt(rho_r * (0.5 * (gamma_gas + 1.0) * pstar + 0.5 * (gamma_gas - 1.0) * p_r))
        z_l = 2.0 * w_l ** 3 / (w_l * w_l + c_l * c_l)
        z_r = 2.0 * w_r ** 3 / (w_r * w_r + c_r * c_r)
        ustar_l = un_l - (pstar - p_l) / w_l
        ustar_r = un_r + (pstar - p_r) / w_r
        pstar = jnp.maximum(pstar - z_l * z_r * (ustar_r - ustar_l) / (z_l + z_r), floor_p)
    w_l = jnp.sqrt(rho_l * (0.5 * (gamma_gas + 1.0) * pstar + 0.5 * (gamma_gas - 1.0) * p_l))
    w_r = jnp.sqrt(rho_r * (0.5 * (gamma_gas + 1.0) * pstar + 0.5 * (gamma_gas - 1.0) * p_r))
    ustar = 0.5 * (un_l - (pstar - p_l) / w_l + (un_r + (pstar - p_r) / w_r))
    return (pstar, ustar)

def sweep(state, axis, normal, ratio):
    rho = state[0]
    mom_n = state[1 + normal]
    mom_t = state[2 - normal]
    energy = state[3]
    un = mom_n / rho
    ut = mom_t / rho
    pres = (gamma_gas - 1.0) * (energy - (mom_n * mom_n + mom_t * mom_t) / (2.0 * rho))
    rho_l, rho_r = reconstruct(rho, axis)
    un_l, un_r = reconstruct(un, axis)
    ut_l, ut_r = reconstruct(ut, axis)
    p_l, p_r = reconstruct(pres, axis)
    pstar, ustar = riemann(rho_l, un_l, p_l, rho_r, un_r, p_r)
    e_l = p_l / (gamma_gas - 1.0) + 0.5 * rho_l * (un_l * un_l + ut_l * ut_l)
    e_r = p_r / (gamma_gas - 1.0) + 0.5 * rho_r * (un_r * un_r + ut_r * ut_r)
    s_plus = jnp.maximum(ustar, 0.0)
    s_minus = jnp.minimum(ustar, 0.0)
    flux_mass = s_plus * rho_l + s_minus * rho_r
    flux_n = flux_mass * ustar + pstar
    flux_t = s_plus * rho_l * ut_l + s_minus * rho_r * ut_r
    flux_e = s_plus * e_l + s_minus * e_r + pstar * ustar

    def update(value, flux):
        return value - ratio * (flux - jnp.roll(flux, 1, axis))
    new_rho = update(rho, flux_mass)
    new_n = update(mom_n, flux_n)
    new_t = update(mom_t, flux_t)
    new_e = update(energy, flux_e)
    if normal == 0:
        return jnp.stack([new_rho, new_n, new_t, new_e])
    return jnp.stack([new_rho, new_t, new_n, new_e])

def reference(density, velocity, pressure):
    mom_x = density * velocity[0]
    mom_y = density * velocity[1]
    energy = pressure / (gamma_gas - 1.0) + 0.5 * density * (velocity[0] * velocity[0] + velocity[1] * velocity[1])
    state = jnp.stack([density, mom_x, mom_y, energy])
    state = sweep(state, 2, 0, 0.025)
    state = sweep(state, 1, 1, 0.05)
    state = sweep(state, 2, 0, 0.025)
    rho = state[0]
    new_velocity = jnp.stack([state[1] / rho, state[2] / rho])
    new_pressure = (gamma_gas - 1.0) * (state[3] - (state[1] * state[1] + state[2] * state[2]) / (2.0 * rho))
    return (rho, new_velocity, new_pressure)
```

```python
import jax
import jax.numpy as jnp
from jax import lax
from jax.experimental import pallas as pl
from jax.experimental.pallas import tpu as pltpu
from jax.sharding import PartitionSpec as P

MESH = pl.DeviceIdType.MESH
NEWTON = 4
LANES = 128
ROWS = 8
QUARTER = 8
HALO = 3
GROUP = 3


def inverse(value):
    return pl.reciprocal(value, approx=False)


def column_shift(values, step):
    lane = lax.broadcasted_iota(jnp.int32, values.shape, 2)
    if step == 1:
        turned = pltpu.roll(values, LANES - 1, 2)
        other = jnp.concatenate([turned[1:], turned[-1:]], axis=0)
        return jnp.where(lane == LANES - 1, other, turned)
    turned = pltpu.roll(values, 1, 2)
    other = jnp.concatenate([turned[:1], turned[:-1]], axis=0)
    return jnp.where(lane == 0, other, turned)


def limited(values, dr, dl):
    two_r = 2.0 * jnp.abs(dr)
    two_l = 2.0 * jnp.abs(dl)
    left = values + jnp.minimum(jnp.maximum(dr, -two_l), two_l)
    right = values + jnp.minimum(jnp.maximum(dl, -two_r), two_r)
    return left, right


def half_step(d, d_before, d_after):
    raw = 0.5 * d + (d_before - d_after) * (1.0 / 12.0)
    return jnp.minimum(jnp.maximum(raw, jnp.minimum(d, 0.0)), jnp.maximum(d, 0.0))


def edges_along_columns(values):
    d = column_shift(values, 1) - values
    dr = half_step(d, column_shift(d, -1), column_shift(d, 1))
    dl = column_shift(dr - d, -1)
    left, right = limited(values, dr, dl)
    return left[:-1], column_shift(right, 1)[:-1]


def edges_along_rows(values):
    d = values[1:] - values[:-1]
    dr = half_step(d[1:-1], d[:-2], d[2:])
    back = dr - d[1:-1]
    left, right = limited(values[2:12], dr[1:], back[:-1])
    return left[:-1], right[1:]


def fluxes(left, right, ratio):
    rho_l, un_l, ut_l, p_l = left
    rho_r, un_r, ut_r, p_r = right
    b_l = 0.2 * rho_l * p_l
    b_r = 0.2 * rho_r * p_r
    a_l = 1.2 * rho_l
    a_r = 1.2 * rho_r
    c_l = 3.5 * b_l
    c_r = 3.5 * b_r
    du = un_l - un_r
    inv_l = lax.rsqrt(7.0 * b_l)
    inv_r = lax.rsqrt(7.0 * b_r)
    floor_p = 0.1 * jnp.minimum(p_l, p_r)
    pstar = (p_l * inv_l + p_r * inv_r + du) * inverse(inv_l + inv_r)
    pstar = jnp.maximum(pstar, floor_p)
    for _ in range(NEWTON):
        s_l = lax.rsqrt(a_l * pstar + b_l)
        s_r = lax.rsqrt(a_r * pstar + b_r)
        slope = s_l * (0.5 + c_l * (s_l * s_l)) + s_r * (0.5 + c_r * (s_r * s_r))
        gap = (pstar - p_l) * s_l + (pstar - p_r) * s_r - du
        pstar = jnp.maximum(pstar - gap * inverse(slope), floor_p)
    s_l = lax.rsqrt(a_l * pstar + b_l)
    s_r = lax.rsqrt(a_r * pstar + b_r)
    ustar = 0.5 * ((un_l + un_r) + ((pstar - p_r) * s_r - (pstar - p_l) * s_l))
    from_left = ustar >= 0.0
    rho = jnp.where(from_left, rho_l, rho_r)
    un = jnp.where(from_left, un_l, un_r)
    ut = jnp.where(from_left, ut_l, ut_r)
    p = jnp.where(from_left, p_l, p_r)
    u_r = ratio * ustar
    mass = u_r * rho
    normal = mass * ustar + ratio * pstar
    trans = mass * ut
    energy = u_r * (2.5 * p + pstar) + 0.5 * mass * (un * un + ut * ut)
    return mass, normal, trans, energy


def primitives(rho, mx, my, energy):
    inv = inverse(rho)
    u = mx * inv
    v = my * inv
    p = 0.4 * (energy - 0.5 * (mx * u + my * v))
    return u, v, p


def face_fluxes(edge_ref, flux_ref, ratio):
    for first in range(0, QUARTER + 1, GROUP):
        part = pl.ds(first, GROUP)
        left = tuple(edge_ref[f, 0, part] for f in range(4))
        right = tuple(edge_ref[f, 1, part] for f in range(4))
        for f, flux in enumerate(fluxes(left, right, ratio)):
            flux_ref[f, part] = flux


def kernel(
    density, velocity, pressure, new_density, new_velocity, new_pressure,
    start, first, second, final, edge, flux, to_up, to_down, from_up, from_down,
    in_sem, out_sem, send_sem, recv_sem,
):
    slab = lax.axis_index("slab")
    me = lax.axis_index("pencil")
    count = lax.axis_size("pencil")
    up = lax.rem(me + 1, count)
    down = lax.rem(me + count - 1, count)
    planes, blocks = start.shape[1], start.shape[2]
    quarters = blocks // QUARTER
    units = planes * quarters

    barrier = pltpu.get_barrier_semaphore()
    for neighbour in (up, down):
        pl.semaphore_signal(barrier, inc=1, device_id=(slab, neighbour), device_id_type=MESH)

    def sources(plane):
        return (density.at[plane], velocity.at[0, plane], velocity.at[1, plane], pressure.at[plane])

    def load(plane, f):
        return pltpu.make_async_copy(sources(plane)[f], start.at[f, plane], in_sem.at[f, plane])

    for plane in range(planes):
        for f in range(4):
            load(plane, f).start()

    def around(quarter):
        before = lax.rem(quarter * QUARTER + blocks - 1, blocks)
        after = lax.rem(quarter * QUARTER + QUARTER, blocks)
        return before, quarter * QUARTER, after

    def column_sweep(quarter, read, conserved, write, ratio):
        before, own, after = around(quarter)
        for f in range(4):
            values = jnp.concatenate([read(f, before, 1), read(f, own, QUARTER), read(f, after, 1)], axis=0)
            left, right = edges_along_columns(values)
            edge[f, 0] = left
            edge[f, 1] = right
        face_fluxes(edge, flux, ratio)
        changed = []
        for f, old in enumerate(conserved(own)):
            here = flux[f]
            changed.append(old - (here - column_shift(here, -1))[1:])
        write(own, changed)

    def copy_up(unit):
        return pltpu.make_async_remote_copy(
            to_up.at[unit], from_down.at[unit], send_sem.at[0, unit], recv_sem.at[0, unit],
            device_id=(slab, up), device_id_type=MESH,
        )

    def copy_down(unit):
        return pltpu.make_async_remote_copy(
            to_down.at[unit], from_up.at[unit], send_sem.at[1, unit], recv_sem.at[1, unit],
            device_id=(slab, down), device_id_type=MESH,
        )

    def rows_of(ref, f, plane, block):
        return ref[f, plane, pl.ds(pl.multiple_of(block * ROWS, ROWS), ROWS)]

    def line(quarter, row):
        return pl.ds(quarter * (QUARTER * ROWS) + row, QUARTER, stride=ROWS)

    def first_sweep(unit, carry):
        plane, quarter = unit // quarters, lax.rem(unit, quarters)

        @pl.when(quarter == 0)
        def _():
            for f in range(4):
                load(plane, f).wait()

        def read(f, block, n):
            return start[f, plane, pl.ds(block, n)]

        def conserved(own):
            rho, u, v, p = (read(f, own, QUARTER) for f in range(4))
            mx = rho * u
            my = rho * v
            return rho, mx, my, 2.5 * p + 0.5 * (mx * u + my * v)

        def write(own, changed):
            rho, mx, my, energy = changed
            u, v, p = primitives(rho, mx, my, energy)
            here = pl.ds(pl.multiple_of(own * ROWS, QUARTER * ROWS), QUARTER * ROWS)
            for f, value in enumerate((rho, u, v, p, mx, my, energy)):
                first[f, plane, here] = value.reshape(QUARTER * ROWS, LANES)

        column_sweep(quarter, read, conserved, write, 0.025)
        for f in range(4):
            for row in range(HALO):
                to_up[unit, f * HALO + row] = first[f, plane, line(quarter, ROWS - HALO + row)]
                to_down[unit, f * HALO + row] = first[f, plane, line(quarter, row)]

        @pl.when(unit == 0)
        def _():
            pl.semaphore_wait(barrier, 2)

        copy_up(unit).start()
        copy_down(unit).start()
        return carry

    lax.fori_loop(0, units, first_sweep, 0)

    def row_sweep(unit):
        plane, quarter = unit // quarters, lax.rem(unit, quarters)
        copy_up(unit).wait_recv()
        copy_down(unit).wait_recv()
        for place, f in enumerate((0, 2, 1, 3)):
            values = jnp.concatenate(
                [from_down[unit, pl.ds(f * HALO, HALO)]]
                + [first[f, plane, line(quarter, row)][None] for row in range(ROWS)]
                + [from_up[unit, pl.ds(f * HALO, HALO)]],
                axis=0,
            )
            left, right = edges_along_rows(values)
            edge[place, 0] = left
            edge[place, 1] = right
        face_fluxes(edge, flux, 0.05)
        mass, normal, trans, energy = (flux[f][1:] - flux[f][:-1] for f in range(4))
        rho, mx, my, en = (
            jnp.stack([first[f, plane, line(quarter, row)] for row in range(ROWS)]) for f in (0, 4, 5, 6)
        )
        rho = rho - mass
        mx = mx - trans
        my = my - normal
        en = en - energy
        u, v, p = primitives(rho, mx, my, en)
        for f, value in enumerate((rho, u, v, p, mx, my, en)):
            for row in range(ROWS):
                second[f, plane, line(quarter, row)] = value[row]

    def store(unit, f):
        plane, quarter = unit // quarters, lax.rem(unit, quarters)
        part = pl.ds(quarter * QUARTER, QUARTER)
        target = (
            new_density.at[plane, part], new_velocity.at[0, plane, part],
            new_velocity.at[1, plane, part], new_pressure.at[plane, part],
        )[f]
        return pltpu.make_async_copy(final.at[f, plane, part], target, out_sem.at[f, unit])

    def last_sweep(unit):
        plane, quarter = unit // quarters, lax.rem(unit, quarters)

        def read(f, block, n):
            here = pl.ds(pl.multiple_of(block * ROWS, ROWS), n * ROWS)
            return second[f, plane, here].reshape(n, ROWS, LANES)

        def conserved(own):
            return tuple(read(f, own, QUARTER) for f in (0, 4, 5, 6))

        def write(own, changed):
            rho, mx, my, energy = changed
            u, v, p = primitives(rho, mx, my, energy)
            for f, value in enumerate((rho, u, v, p)):
                final[f, plane, pl.ds(own, QUARTER)] = value

        column_sweep(quarter, read, conserved, write, 0.025)
        for f in range(4):
            store(unit, f).start()

    def later(unit, carry):
        @pl.when(unit < units)
        def _():
            row_sweep(unit)

        @pl.when(unit >= quarters)
        def _():
            last_sweep(unit - quarters)

        return carry

    lax.fori_loop(0, units + quarters, later, 0)

    def finish(unit, carry):
        copy_up(unit).wait_send()
        copy_down(unit).wait_send()
        for f in range(4):
            store(unit, f).wait()
        return carry

    lax.fori_loop(0, units, finish, 0)


def on_device(density, velocity, pressure):
    planes, rows, columns = density.shape
    blocks = columns // LANES
    units = planes * blocks // QUARTER

    def blocked(a):
        lead = a.shape[:-2]
        return jnp.swapaxes(a.reshape(*lead, rows, blocks, LANES), -3, -2)

    def unblocked(a):
        lead = a.shape[:-3]
        return jnp.swapaxes(a, -3, -2).reshape(*lead, rows, columns)

    any_space = pl.BlockSpec(memory_space=pl.ANY)
    shape = (planes, blocks, rows, LANES)
    f32 = jnp.float32
    halo = (units, 4 * HALO, QUARTER, LANES)
    outs = pl.pallas_call(
        kernel,
        out_shape=(
            jax.ShapeDtypeStruct(shape, f32),
            jax.ShapeDtypeStruct((2, *shape), f32),
            jax.ShapeDtypeStruct(shape, f32),
        ),
        in_specs=[any_space] * 3,
        out_specs=(any_space,) * 3,
        scratch_shapes=[
            pltpu.VMEM((4, *shape), f32),
            pltpu.VMEM((7, planes, blocks * rows, LANES), f32),
            pltpu.VMEM((7, planes, blocks * rows, LANES), f32),
            pltpu.VMEM((4, *shape), f32),
            pltpu.VMEM((4, 2, QUARTER + 1, rows, LANES), f32),
            pltpu.VMEM((4, QUARTER + 1, rows, LANES), f32),
            pltpu.VMEM(halo, f32),
            pltpu.VMEM(halo, f32),
            pltpu.VMEM(halo, f32),
            pltpu.VMEM(halo, f32),
            pltpu.SemaphoreType.DMA((4, planes)),
            pltpu.SemaphoreType.DMA((4, units)),
            pltpu.SemaphoreType.DMA((2, units)),
            pltpu.SemaphoreType.DMA((2, units)),
        ],
        compiler_params=pltpu.CompilerParams(
            collective_id=0, has_side_effects=True, vmem_limit_bytes=48 * 2**20
        ),
    )(blocked(density), blocked(velocity), blocked(pressure))
    return tuple(unblocked(a) for a in outs)


def solution(mesh):
    one = P("slab", "pencil", None)
    two = P(None, "slab", "pencil", None)
    return jax.shard_map(on_device, mesh=mesh, in_specs=(one, two, one), out_specs=(one, two, one), check_vma=False)
```

```python
import jax
import jax.numpy as jnp
from jax import lax
from jax.experimental import pallas as pl
from jax.experimental.pallas import tpu as pltpu
from jax.sharding import PartitionSpec as P

MESH = pl.DeviceIdType.MESH
NEWTON = 4
LANES = 128
ROWS = 8
QUARTER = 8
HALO = 3
LINE = 32
PIECES = LANES // LINE
SIDES = 2
FACES = 11


def inverse(value):
    return pl.reciprocal(value, approx=False)


def edges(values):
    d = values[1:] - values[:-1]
    here = d[1:-1]
    size = jnp.abs(here)
    sign = jnp.where(here >= 0.0, 1.0, -1.0)
    raw = 0.5 * size + sign * ((d[:-2] - d[2:]) * (1.0 / 12.0))
    to_face = jnp.minimum(jnp.maximum(raw, 0.0), size)
    beyond = size - to_face
    cells = values[2:-2]
    left = cells + sign[1:] * jnp.minimum(to_face[1:], 2.0 * beyond[:-1])
    right = cells - sign[:-1] * jnp.minimum(beyond[:-1], 2.0 * to_face[1:])
    return left[:-1], right[1:]


def fluxes(left, right, ratio):
    rho_l, un_l, ut_l, p_l = left
    rho_r, un_r, ut_r, p_r = right
    a_l = 1.2 * rho_l
    a_r = 1.2 * rho_r
    cc_l = (1.4 * rho_l) * p_l
    cc_r = (1.4 * rho_r) * p_r
    h_l = 0.5 * cc_l
    h_r = 0.5 * cc_r
    du = un_l - un_r
    dp = p_l - p_r
    inv_l = lax.rsqrt(cc_l)
    inv_r = lax.rsqrt(cc_r)
    e_r = cc_r + a_r * dp
    floor_y = 0.1 * jnp.minimum(p_l, p_r) - p_l
    y = (du - dp * inv_r) * inverse(inv_l + inv_r)
    y = jnp.maximum(y, floor_y)
    for _ in range(NEWTON):
        s_l = lax.rsqrt(a_l * y + cc_l)
        s_r = lax.rsqrt(a_r * y + e_r)
        slope = s_l * (0.5 + h_l * (s_l * s_l)) + s_r * (0.5 + h_r * (s_r * s_r))
        gap = y * s_l + ((y + dp) * s_r - du)
        y = jnp.maximum(y - gap * inverse(slope), floor_y)
    s_l = lax.rsqrt(a_l * y + cc_l)
    s_r = lax.rsqrt(a_r * y + e_r)
    pstar = y + p_l
    ustar = 0.5 * ((un_l + un_r) + ((y + dp) * s_r - y * s_l))
    from_left = ustar >= 0.0
    rho = jnp.where(from_left, rho_l, rho_r)
    un = jnp.where(from_left, un_l, un_r)
    ut = jnp.where(from_left, ut_l, ut_r)
    p = jnp.where(from_left, p_l, p_r)
    u_r = ratio * ustar
    mass = u_r * rho
    normal = mass * ustar + ratio * pstar
    trans = mass * ut
    energy = u_r * (2.5 * p + pstar) + (0.5 * mass) * (un * un + ut * ut)
    return mass, normal, trans, energy


def updated(cells, change):
    rho, un, ut, p = cells
    mass, normal, trans, lost = change
    mn = rho * un
    mt = rho * ut
    energy = 2.5 * p + 0.5 * (mn * un + mt * ut)
    rho = rho - mass
    mn = mn - normal
    mt = mt - trans
    energy = energy - lost
    inv = inverse(rho)
    un = mn * inv
    ut = mt * inv
    return rho, un, ut, 0.4 * energy - 0.2 * (mn * un + mt * ut)


def turn_in(source, turned):
    for f in range(4):
        for side in range(SIDES):
            across = source(f, side).T
            for piece in range(PIECES):
                for k in range(LINE // ROWS):
                    at = piece * LINE + k * ROWS
                    turned[f, pl.ds((HALO + k * ROWS) * ROWS + side * PIECES + piece, ROWS, stride=ROWS)] = across[at : at + ROWS]
    shape = (ROWS, LANES)
    row = lax.broadcasted_iota(jnp.int32, shape, 0)
    piece = row & (PIECES - 1)
    lane = lax.broadcasted_iota(jnp.int32, shape, 1)
    for f in range(4):
        for k in range(HALO):
            v = turned[f, pl.ds((LINE + k) * ROWS, ROWS)]
            w = pltpu.roll(v, ROWS, 1)
            seam = jnp.where(lane < ROWS, pltpu.roll(w, 1, 0), pltpu.roll(w, 5, 0))
            turned[f, pl.ds(k * ROWS, ROWS)] = jnp.where(piece == 0, seam, pltpu.roll(v, 1, 0))
            v = turned[f, pl.ds((HALO + k) * ROWS, ROWS)]
            w = pltpu.roll(v, LANES - ROWS, 1)
            seam = jnp.where(lane >= LANES - ROWS, pltpu.roll(w, 7, 0), pltpu.roll(w, 3, 0))
            turned[f, pl.ds((HALO + LINE + k) * ROWS, ROWS)] = jnp.where(piece == PIECES - 1, seam, pltpu.roll(v, 7, 0))


def turn_out(turned, target):
    for f in range(4):
        for side in range(SIDES):
            parts = [
                turned[f, pl.ds((1 + k * ROWS) * ROWS + side * PIECES + piece, ROWS, stride=ROWS)]
                for piece in range(PIECES)
                for k in range(LINE // ROWS)
            ]
            target(f, side, jnp.concatenate(parts, axis=0).T)


def column_sweep(source, target, turned, swept, ratio):
    turn_in(source, turned)

    def some(part, last):
        at = pl.multiple_of(part * (FACES * ROWS), ROWS)
        cells = [
            turned[f, pl.ds(at, (FACES + 5) * ROWS)].reshape(FACES + 5, ROWS, LANES) for f in range(4)
        ]
        sides = [edges(c) for c in cells]
        flux = fluxes([s[0] for s in sides], [s[1] for s in sides], ratio)
        change = [now - jnp.concatenate([old, now[:-1]], axis=0) for now, old in zip(flux, last)]
        for f, value in enumerate(updated([c[2:-3] for c in cells], change)):
            swept[f, pl.ds(at, FACES * ROWS)] = value.reshape(FACES * ROWS, LANES)
        return tuple(now[-1:] for now in flux)

    none = jnp.zeros((1, ROWS, LANES), jnp.float32)
    lax.fori_loop(0, (LINE + 1) // FACES, some, (none,) * 4)
    turn_out(swept, target)


def kernel(
    density, velocity, pressure, new_density, new_velocity, new_pressure,
    start, first, second, final, turned, swept, to_up, to_down, from_up, from_down,
    in_sem, out_sem, send_sem, recv_sem, ready_sem,
):
    slab = lax.axis_index("slab")
    me = lax.axis_index("pencil")
    count = lax.axis_size("pencil")
    up = lax.rem(me + 1, count)
    down = lax.rem(me + count - 1, count)
    planes = start.shape[1]
    quarters = start.shape[2] // (QUARTER * ROWS)
    units = planes * quarters

    barrier = pltpu.get_barrier_semaphore()
    pl.semaphore_signal(barrier, inc=1, device_id=(slab, down), device_id_type=MESH)

    def load(plane, f):
        source = (density.at[plane], velocity.at[0, plane], velocity.at[1, plane], pressure.at[plane])[f]
        return pltpu.make_async_copy(source, start.at[f, plane], in_sem.at[f, plane])

    for plane in range(planes):
        for f in range(4):
            load(plane, f).start()

    def half(ref, plane):
        return lambda f, side: ref[f, plane, pl.ds(side * LANES, LANES)]

    def into(ref, plane):
        def put(f, side, value):
            ref[f, plane, pl.ds(side * LANES, LANES)] = value

        return put

    def copy_up(unit):
        return pltpu.make_async_remote_copy(
            to_up.at[unit], from_down.at[unit], send_sem.at[0, unit], recv_sem.at[0, unit],
            device_id=(slab, up), device_id_type=MESH,
        )

    def copy_down(unit):
        return pltpu.make_async_remote_copy(
            to_down.at[unit], from_up.at[unit], send_sem.at[1, unit], recv_sem.at[1, unit],
            device_id=(slab, down), device_id_type=MESH,
        )

    def line(quarter, row):
        return pl.ds(quarter * (QUARTER * ROWS) + row, QUARTER, stride=ROWS)

    def first_sweep(plane, carry):
        for f in range(4):
            load(plane, f).wait()
        column_sweep(half(start, plane), into(first, plane), turned, swept, 0.025)
        for quarter in range(quarters):
            unit = plane * quarters + quarter
            for f in range(4):
                for row in range(HALO):
                    to_up[unit, f * HALO + row] = first[f, plane, line(quarter, ROWS - HALO + row)]
                    to_down[unit, f * HALO + row] = first[f, plane, line(quarter, row)]

        @pl.when(plane == 0)
        def _():
            pl.semaphore_wait(barrier, 1)
            pl.semaphore_signal(ready_sem, inc=1, device_id=(slab, up), device_id_type=MESH)

        for quarter in range(quarters):
            copy_up(plane * quarters + quarter).start()
        return carry

    lax.fori_loop(0, planes, first_sweep, 0)
    pl.semaphore_wait(ready_sem, 1)

    def send_down(unit, carry):
        copy_down(unit).start()
        return carry

    lax.fori_loop(0, units, send_down, 0)

    def row_sweep(unit):
        plane, quarter = unit // quarters, lax.rem(unit, quarters)
        copy_up(unit).wait_recv()
        copy_down(unit).wait_recv()
        sides, cells = [], []
        for f in (0, 2, 1, 3):
            own = [first[f, plane, line(quarter, row)][None] for row in range(ROWS)]
            below = from_down[unit, pl.ds(f * HALO, HALO)]
            above = from_up[unit, pl.ds(f * HALO, HALO)]
            sides.append(edges(jnp.concatenate([below, *own, above], axis=0)))
            cells.append(jnp.concatenate(own, axis=0))
        flux = fluxes([s[0] for s in sides], [s[1] for s in sides], 0.05)
        new = updated(cells, [now[1:] - now[:-1] for now in flux])
        for f, value in zip((0, 2, 1, 3), new):
            for row in range(ROWS):
                second[f, plane, line(quarter, row)] = value[row]

    def store(plane, f):
        target = (
            new_density.at[plane], new_velocity.at[0, plane], new_velocity.at[1, plane], new_pressure.at[plane],
        )[f]
        return pltpu.make_async_copy(final.at[f, plane], target, out_sem.at[f, plane])

    def later(plane, carry):
        def row_sweeps(quarter, inner):
            row_sweep(plane * quarters + quarter)
            return inner

        lax.fori_loop(0, quarters, row_sweeps, 0)
        column_sweep(half(second, plane), into(final, plane), turned, swept, 0.025)
        for f in range(4):
            store(plane, f).start()
        return carry

    lax.fori_loop(0, planes, later, 0)

    def sent(unit, carry):
        copy_up(unit).wait_send()
        copy_down(unit).wait_send()
        return carry

    lax.fori_loop(0, units, sent, 0)
    for plane in range(planes):
        for f in range(4):
            store(plane, f).wait()


def on_device(density, velocity, pressure):
    planes, rows, columns = density.shape
    blocks = columns // LANES
    units = planes * blocks // QUARTER

    def blocked(a):
        lead = a.shape[:-2]
        return jnp.swapaxes(a.reshape(*lead, rows, blocks, LANES), -3, -2).reshape(*lead, blocks * rows, LANES)

    def unblocked(a):
        lead = a.shape[:-2]
        return jnp.swapaxes(a.reshape(*lead, blocks, rows, LANES), -3, -2).reshape(*lead, rows, columns)

    hbm = pl.BlockSpec(memory_space=pltpu.HBM)
    shape = (planes, blocks * rows, LANES)
    f32 = jnp.float32
    halo = (units, 4 * HALO, QUARTER, LANES)
    outs = pl.pallas_call(
        kernel,
        out_shape=(
            jax.ShapeDtypeStruct(shape, f32),
            jax.ShapeDtypeStruct((2, *shape), f32),
            jax.ShapeDtypeStruct(shape, f32),
        ),
        in_specs=[hbm] * 3,
        out_specs=(hbm,) * 3,
        scratch_shapes=[
            pltpu.VMEM((4, *shape), f32),
            pltpu.VMEM((4, *shape), f32),
            pltpu.VMEM((4, *shape), f32),
            pltpu.VMEM((4, *shape), f32),
            pltpu.VMEM((4, (LINE + 2 * HALO) * ROWS, LANES), f32),
            pltpu.VMEM((4, (LINE + 1) * ROWS, LANES), f32),
            pltpu.VMEM(halo, f32),
            pltpu.VMEM(halo, f32),
            pltpu.VMEM(halo, f32),
            pltpu.VMEM(halo, f32),
            pltpu.SemaphoreType.DMA((4, planes)),
            pltpu.SemaphoreType.DMA((4, planes)),
            pltpu.SemaphoreType.DMA((2, units)),
            pltpu.SemaphoreType.DMA((2, units)),
            pltpu.SemaphoreType.REGULAR,
        ],
        compiler_params=pltpu.CompilerParams(
            collective_id=0, has_side_effects=True, vmem_limit_bytes=48 * 2**20
        ),
    )(*(pltpu.with_memory_space_constraint(blocked(a), pltpu.HBM) for a in (density, velocity, pressure)))
    return tuple(unblocked(a) for a in outs)


def solution(mesh):
    one = P("slab", "pencil", None)
    two = P(None, "slab", "pencil", None)
    return jax.shard_map(on_device, mesh=mesh, in_specs=(one, two, one), out_specs=(one, two, one), check_vma=False)
```

```python
import jax
import jax.numpy as jnp
from jax import lax
from jax.experimental import pallas as pl
from jax.experimental.pallas import tpu as pltpu
from jax.sharding import PartitionSpec as P

MESH = pl.DeviceIdType.MESH
NEWTON = 4
LANES = 128
ROWS = 8
QUARTER = 8
HALO = 3
LINE = 32
PIECES = LANES // LINE
SIDES = 2
FACES = 11


def inverse(value):
    return pl.reciprocal(value, approx=False)


def edges(values):
    d = values[1:] - values[:-1]
    here = d[1:-1]
    size = jnp.abs(here)
    sign = jnp.where(here >= 0.0, 1.0, -1.0)
    raw = 0.5 * size + sign * ((d[:-2] - d[2:]) * (1.0 / 12.0))
    to_face = jnp.minimum(jnp.maximum(raw, 0.0), size)
    beyond = size - to_face
    cells = values[2:-2]
    left = cells + sign[1:] * jnp.minimum(to_face[1:], 2.0 * beyond[:-1])
    right = cells - sign[:-1] * jnp.minimum(beyond[:-1], 2.0 * to_face[1:])
    return left[:-1], right[1:]


def fluxes(left, right, ratio):
    rho_l, un_l, ut_l, p_l = left
    rho_r, un_r, ut_r, p_r = right
    a_l = 1.2 * rho_l
    a_r = 1.2 * rho_r
    cc_l = (1.4 * rho_l) * p_l
    cc_r = (1.4 * rho_r) * p_r
    h_l = 0.5 * cc_l
    h_r = 0.5 * cc_r
    du = un_l - un_r
    dp = p_l - p_r
    inv_l = lax.rsqrt(cc_l)
    inv_r = lax.rsqrt(cc_r)
    e_r = cc_r + a_r * dp
    floor_y = 0.1 * jnp.minimum(p_l, p_r) - p_l
    y = (du - dp * inv_r) * inverse(inv_l + inv_r)
    y = jnp.maximum(y, floor_y)
    for _ in range(NEWTON):
        s_l = lax.rsqrt(a_l * y + cc_l)
        s_r = lax.rsqrt(a_r * y + e_r)
        slope = s_l * (0.5 + h_l * (s_l * s_l)) + s_r * (0.5 + h_r * (s_r * s_r))
        gap = y * s_l + ((y + dp) * s_r - du)
        y = jnp.maximum(y - gap * inverse(slope), floor_y)
    s_l = lax.rsqrt(a_l * y + cc_l)
    s_r = lax.rsqrt(a_r * y + e_r)
    pstar = y + p_l
    ustar = 0.5 * ((un_l + un_r) + ((y + dp) * s_r - y * s_l))
    from_left = ustar >= 0.0
    rho = jnp.where(from_left, rho_l, rho_r)
    un = jnp.where(from_left, un_l, un_r)
    ut = jnp.where(from_left, ut_l, ut_r)
    p = jnp.where(from_left, p_l, p_r)
    u_r = ratio * ustar
    mass = u_r * rho
    normal = mass * ustar + ratio * pstar
    trans = mass * ut
    energy = u_r * (2.5 * p + pstar) + (0.5 * mass) * (un * un + ut * ut)
    return mass, normal, trans, energy


def updated(cells, change):
    rho, un, ut, p = cells
    mass, normal, trans, lost = change
    mn = rho * un
    mt = rho * ut
    energy = 2.5 * p + 0.5 * (mn * un + mt * ut)
    rho = rho - mass
    mn = mn - normal
    mt = mt - trans
    energy = energy - lost
    inv = inverse(rho)
    un = mn * inv
    ut = mt * inv
    return rho, un, ut, 0.4 * energy - 0.2 * (mn * un + mt * ut)


def turn_in(source, turned):
    for f in range(4):
        for side in range(SIDES):
            across = source(f, side).T
            for piece in range(PIECES):
                for k in range(LINE // ROWS):
                    at = piece * LINE + k * ROWS
                    turned[f, pl.ds((HALO + k * ROWS) * ROWS + side * PIECES + piece, ROWS, stride=ROWS)] = across[at : at + ROWS]
    shape = (ROWS, LANES)
    row = lax.broadcasted_iota(jnp.int32, shape, 0)
    piece = row & (PIECES - 1)
    lane = lax.broadcasted_iota(jnp.int32, shape, 1)
    for f in range(4):
        for k in range(HALO):
            v = turned[f, pl.ds((LINE + k) * ROWS, ROWS)]
            w = pltpu.roll(v, ROWS, 1)
            seam = jnp.where(lane < ROWS, pltpu.roll(w, 1, 0), pltpu.roll(w, 5, 0))
            turned[f, pl.ds(k * ROWS, ROWS)] = jnp.where(piece == 0, seam, pltpu.roll(v, 1, 0))
            v = turned[f, pl.ds((HALO + k) * ROWS, ROWS)]
            w = pltpu.roll(v, LANES - ROWS, 1)
            seam = jnp.where(lane >= LANES - ROWS, pltpu.roll(w, 7, 0), pltpu.roll(w, 3, 0))
            turned[f, pl.ds((HALO + LINE + k) * ROWS, ROWS)] = jnp.where(piece == PIECES - 1, seam, pltpu.roll(v, 7, 0))


def turn_out(turned, target):
    for f in range(4):
        for side in range(SIDES):
            parts = [
                turned[f, pl.ds((1 + k * ROWS) * ROWS + side * PIECES + piece, ROWS, stride=ROWS)]
                for piece in range(PIECES)
                for k in range(LINE // ROWS)
            ]
            target(f, side, jnp.concatenate(parts, axis=0).T)


def column_sweep(source, target, turned, swept, ratio):
    turn_in(source, turned)

    def some(part, last):
        at = pl.multiple_of(part * (FACES * ROWS), ROWS)
        cells = [
            turned[f, pl.ds(at, (FACES + 5) * ROWS)].reshape(FACES + 5, ROWS, LANES) for f in range(4)
        ]
        sides = [edges(c) for c in cells]
        flux = fluxes([s[0] for s in sides], [s[1] for s in sides], ratio)
        change = [now - jnp.concatenate([old, now[:-1]], axis=0) for now, old in zip(flux, last)]
        for f, value in enumerate(updated([c[2:-3] for c in cells], change)):
            swept[f, pl.ds(at, FACES * ROWS)] = value.reshape(FACES * ROWS, LANES)
        return tuple(now[-1:] for now in flux)

    none = jnp.zeros((1, ROWS, LANES), jnp.float32)
    lax.fori_loop(0, (LINE + 1) // FACES, some, (none,) * 4)
    turn_out(swept, target)


def half(ref, *index):
    return lambda f, side: ref[(f, *index, pl.ds(side * LANES, LANES))]


def into(ref, *index):
    def put(f, side, value):
        ref[(f, *index, pl.ds(side * LANES, LANES))] = value

    return put


def line(quarter, row):
    return pl.ds(quarter * (QUARTER * ROWS) + row, QUARTER, stride=ROWS)


def kernel(
    density, velocity, pressure, done, left,
    start, first, outer, turned, swept, to_up, to_down, from_up, from_down,
    in_sem, send_sem, recv_sem, ready_sem,
):
    slab = lax.axis_index("slab")
    me = lax.axis_index("pencil")
    count = lax.axis_size("pencil")
    up = lax.rem(me + 1, count)
    down = lax.rem(me + count - 1, count)
    planes = start.shape[1]
    quarters = start.shape[2] // (QUARTER * ROWS)

    barrier = pltpu.get_barrier_semaphore()
    pl.semaphore_signal(barrier, inc=1, device_id=(slab, down), device_id_type=MESH)

    def load(plane, f):
        source = (density.at[plane], velocity.at[0, plane], velocity.at[1, plane], pressure.at[plane])[f]
        return pltpu.make_async_copy(source, start.at[f, plane], in_sem.at[f, plane])

    for plane in range(planes):
        for f in range(4):
            load(plane, f).start()

    def copy_up(unit):
        return pltpu.make_async_remote_copy(
            to_up.at[unit], from_down.at[unit], send_sem.at[0, unit], recv_sem.at[0, unit],
            device_id=(slab, up), device_id_type=MESH,
        )

    def copy_down(unit):
        return pltpu.make_async_remote_copy(
            to_down.at[unit], from_up.at[unit], send_sem.at[1, unit], recv_sem.at[1, unit],
            device_id=(slab, down), device_id_type=MESH,
        )

    def pack(ref, plane):
        for quarter in range(quarters):
            unit = plane * quarters + quarter
            for f in range(4):
                for row in range(HALO):
                    to_up[unit, f * HALO + row] = ref[f, plane, line(quarter, ROWS - HALO + row)]
                    to_down[unit, f * HALO + row] = ref[f, plane, line(quarter, row)]

    def send(copy, plane):
        for quarter in range(quarters):
            copy(plane * quarters + quarter).start()

    for f in range(4):
        load(0, f).wait()
    pack(start, 0)
    pl.semaphore_wait(barrier, 1)
    pl.semaphore_signal(ready_sem, inc=1, device_id=(slab, up), device_id_type=MESH)
    send(copy_up, 0)

    def first_sweep(plane, carry):
        @pl.when(plane > 0)
        def _():
            for f in range(4):
                load(plane, f).wait()

        column_sweep(half(start, plane), into(first, plane), turned, swept, 0.025)

        @pl.when(plane > 0)
        def _():
            pack(first, plane)
            send(copy_up, plane)

        @pl.when(plane == 1)
        def _():
            pl.semaphore_wait(ready_sem, 1)

        @pl.when(plane > 0)
        def _():
            send(copy_down, plane - 1)

        @pl.when(plane == planes - 1)
        def _():
            send(copy_down, plane)

        return carry

    lax.fori_loop(0, planes, first_sweep, 0)

    def arrive(unit):
        copy_up(unit).wait_recv()
        copy_down(unit).wait_recv()

    def outer_sweep():
        for quarter in range(quarters):
            arrive(quarter)
            for f in range(4):
                for row in range(HALO):
                    outer[f, line(quarter, row)] = from_down[quarter, f * HALO + row]
                    outer[f, line(quarter, HALO + row)] = from_up[quarter, f * HALO + row]
                for row in range(2 * HALO, ROWS):
                    outer[f, line(quarter, row)] = from_down[quarter, f * HALO]
        column_sweep(half(outer), into(outer), turned, swept, 0.025)
        for quarter in range(quarters):
            for f in range(4):
                for row in range(HALO):
                    from_down[quarter, f * HALO + row] = outer[f, line(quarter, row)]
                    from_up[quarter, f * HALO + row] = outer[f, line(quarter, HALO + row)]

    def row_sweep(plane, quarter):
        unit = plane * quarters + quarter

        @pl.when(plane > 0)
        def _():
            arrive(unit)

        sides, cells = [], []
        for f in (0, 2, 1, 3):
            own = [first[f, plane, line(quarter, row)][None] for row in range(ROWS)]
            below = from_down[unit, pl.ds(f * HALO, HALO)]
            above = from_up[unit, pl.ds(f * HALO, HALO)]
            sides.append(edges(jnp.concatenate([below, *own, above], axis=0)))
            cells.append(jnp.concatenate(own, axis=0))
        flux = fluxes([s[0] for s in sides], [s[1] for s in sides], 0.05)
        new = updated(cells, [now[1:] - now[:-1] for now in flux])
        for f, value in zip((0, 2, 1, 3), new):
            for row in range(ROWS):
                left[f, line(quarter, row)] = value[row]

    def later(plane, carry):
        pl.when(plane == 0)(outer_sweep)

        def row_sweeps(quarter, inner):
            row_sweep(plane, quarter)
            return inner

        lax.fori_loop(0, quarters, row_sweeps, 0)

        @pl.when(plane < planes - 1)
        def _():
            column_sweep(half(left), into(done, plane), turned, swept, 0.025)

        return carry

    lax.fori_loop(0, planes, later, 0)
    def sent(unit, carry):
        copy_up(unit).wait_send()
        copy_down(unit).wait_send()
        return carry

    lax.fori_loop(0, planes * quarters, sent, 0)


def last_kernel(done, left, new_density, new_velocity, new_pressure, final, turned, swept, out_sem):
    before = done.shape[1]

    def store(plane, f):
        target = (
            new_density.at[plane], new_velocity.at[0, plane], new_velocity.at[1, plane], new_pressure.at[plane],
        )[f]
        source = final.at[f] if plane == before else done.at[f, plane]
        return pltpu.make_async_copy(source, target, out_sem.at[f, plane])

    for plane in range(before):
        for f in range(4):
            store(plane, f).start()
    column_sweep(half(left), into(final), turned, swept, 0.025)
    for f in range(4):
        store(before, f).start()
    for plane in range(before + 1):
        for f in range(4):
            store(plane, f).wait()


def on_device(density, velocity, pressure):
    planes, rows, columns = density.shape
    blocks = columns // LANES
    units = planes * blocks // QUARTER

    def blocked(a):
        lead = a.shape[:-2]
        a = jnp.swapaxes(a.reshape(*lead, rows, blocks, LANES), -3, -2).reshape(*lead, blocks * rows, LANES)
        return pltpu.with_memory_space_constraint(a, pltpu.HBM)

    def unblocked(a):
        lead = a.shape[:-2]
        return jnp.swapaxes(a.reshape(*lead, blocks, rows, LANES), -3, -2).reshape(*lead, rows, columns)

    hbm = pl.BlockSpec(memory_space=pltpu.HBM)
    vmem = pl.BlockSpec(memory_space=pltpu.VMEM)
    plane = (blocks * rows, LANES)
    f32 = jnp.float32
    halo = (units, 4 * HALO, QUARTER, LANES)
    work = [
        pltpu.VMEM((4, (LINE + 2 * HALO) * ROWS, LANES), f32),
        pltpu.VMEM((4, (LINE + 1) * ROWS, LANES), f32),
    ]
    done, left = pl.pallas_call(
        kernel,
        out_shape=(pltpu.VMEM((4, planes - 1, *plane), f32), pltpu.VMEM((4, *plane), f32)),
        in_specs=[hbm] * 3,
        out_specs=(vmem, vmem),
        scratch_shapes=[
            pltpu.VMEM((4, planes, *plane), f32),
            pltpu.VMEM((4, planes, *plane), f32),
            pltpu.VMEM((4, *plane), f32),
            *work,
            pltpu.VMEM(halo, f32),
            pltpu.VMEM(halo, f32),
            pltpu.VMEM(halo, f32),
            pltpu.VMEM(halo, f32),
            pltpu.SemaphoreType.DMA((4, planes)),
            pltpu.SemaphoreType.DMA((2, units)),
            pltpu.SemaphoreType.DMA((2, units)),
            pltpu.SemaphoreType.REGULAR,
        ],
        compiler_params=pltpu.CompilerParams(
            collective_id=0, has_side_effects=True, vmem_limit_bytes=32 * 2**20
        ),
    )(blocked(density), blocked(velocity), blocked(pressure))
    outs = pl.pallas_call(
        last_kernel,
        out_shape=(pltpu.HBM((planes, *plane), f32), pltpu.HBM((2, planes, *plane), f32), pltpu.HBM((planes, *plane), f32)),
        in_specs=[vmem] * 2,
        out_specs=(hbm,) * 3,
        scratch_shapes=[pltpu.VMEM((4, *plane), f32), *work, pltpu.SemaphoreType.DMA((4, planes))],
        compiler_params=pltpu.CompilerParams(vmem_limit_bytes=16 * 2**20),
    )(*(pltpu.with_memory_space_constraint(a, pltpu.VMEM) for a in (done, left)))
    return tuple(unblocked(a) for a in outs)


def solution(mesh):
    one = P("slab", "pencil", None)
    two = P(None, "slab", "pencil", None)
    return jax.shard_map(on_device, mesh=mesh, in_specs=(one, two, one), out_specs=(one, two, one), check_vma=False)
```

```python
import jax
import jax.numpy as jnp
from jax import lax
from jax.experimental import pallas as pl
from jax.experimental.pallas import tpu as pltpu
from jax.sharding import PartitionSpec as P

MESH = pl.DeviceIdType.MESH
NEWTON = 4
LANES = 128
ROWS = 8
QUARTER = 8
HALO = 3
GROUP = 8
LINE = 32
PIECES = LANES // LINE
SIDES = 2
FACES = 11


def inverse(value):
    return pl.reciprocal(value, approx=False)


def edges(values):
    d = values[1:] - values[:-1]
    here = d[1:-1]
    size = jnp.abs(here)
    sign = jnp.where(here >= 0.0, 1.0, -1.0)
    raw = 0.5 * size + sign * ((d[:-2] - d[2:]) * (1.0 / 12.0))
    to_face = jnp.minimum(jnp.maximum(raw, 0.0), size)
    beyond = size - to_face
    cells = values[2:-2]
    left = cells + sign[1:] * jnp.minimum(to_face[1:], 2.0 * beyond[:-1])
    right = cells - sign[:-1] * jnp.minimum(beyond[:-1], 2.0 * to_face[1:])
    return left[:-1], right[1:]


def fluxes(left, right, ratio):
    rho_l, un_l, ut_l, p_l = left
    rho_r, un_r, ut_r, p_r = right
    a_l = 1.2 * rho_l
    a_r = 1.2 * rho_r
    cc_l = (1.4 * rho_l) * p_l
    cc_r = (1.4 * rho_r) * p_r
    h_l = 0.5 * cc_l
    h_r = 0.5 * cc_r
    du = un_l - un_r
    dp = p_l - p_r
    inv_l = lax.rsqrt(cc_l)
    inv_r = lax.rsqrt(cc_r)
    e_r = cc_r + a_r * dp
    floor_y = 0.1 * jnp.minimum(p_l, p_r) - p_l
    y = (du - dp * inv_r) * inverse(inv_l + inv_r)
    y = jnp.maximum(y, floor_y)
    for _ in range(NEWTON):
        s_l = lax.rsqrt(a_l * y + cc_l)
        s_r = lax.rsqrt(a_r * y + e_r)
        slope = s_l * (0.5 + h_l * (s_l * s_l)) + s_r * (0.5 + h_r * (s_r * s_r))
        gap = y * s_l + ((y + dp) * s_r - du)
        y = jnp.maximum(y - gap * inverse(slope), floor_y)
    s_l = lax.rsqrt(a_l * y + cc_l)
    s_r = lax.rsqrt(a_r * y + e_r)
    pstar = y + p_l
    ustar = 0.5 * ((un_l + un_r) + ((y + dp) * s_r - y * s_l))
    from_left = ustar >= 0.0
    rho = jnp.where(from_left, rho_l, rho_r)
    un = jnp.where(from_left, un_l, un_r)
    ut = jnp.where(from_left, ut_l, ut_r)
    p = jnp.where(from_left, p_l, p_r)
    u_r = ratio * ustar
    mass = u_r * rho
    normal = mass * ustar + ratio * pstar
    trans = mass * ut
    energy = u_r * (2.5 * p + pstar) + (0.5 * mass) * (un * un + ut * ut)
    return mass, normal, trans, energy


def updated(cells, change):
    rho, un, ut, p = cells
    mass, normal, trans, lost = change
    mn = rho * un
    mt = rho * ut
    energy = 2.5 * p + 0.5 * (mn * un + mt * ut)
    rho = rho - mass
    mn = mn - normal
    mt = mt - trans
    energy = energy - lost
    inv = inverse(rho)
    un = mn * inv
    ut = mt * inv
    return rho, un, ut, 0.4 * energy - 0.2 * (mn * un + mt * ut)


def turn_in(source, turned):
    for f in range(4):
        for side in range(SIDES):
            across = source(f, side).T
            for piece in range(PIECES):
                for k in range(LINE // ROWS):
                    at = piece * LINE + k * ROWS
                    turned[f, pl.ds((HALO + k * ROWS) * ROWS + side * PIECES + piece, ROWS, stride=ROWS)] = across[at : at + ROWS]
    shape = (ROWS, LANES)
    row = lax.broadcasted_iota(jnp.int32, shape, 0)
    piece = row & (PIECES - 1)
    lane = lax.broadcasted_iota(jnp.int32, shape, 1)
    for f in range(4):
        for k in range(HALO):
            v = turned[f, pl.ds((LINE + k) * ROWS, ROWS)]
            w = pltpu.roll(v, ROWS, 1)
            seam = jnp.where(lane < ROWS, pltpu.roll(w, 1, 0), pltpu.roll(w, 5, 0))
            turned[f, pl.ds(k * ROWS, ROWS)] = jnp.where(piece == 0, seam, pltpu.roll(v, 1, 0))
            v = turned[f, pl.ds((HALO + k) * ROWS, ROWS)]
            w = pltpu.roll(v, LANES - ROWS, 1)
            seam = jnp.where(lane >= LANES - ROWS, pltpu.roll(w, 7, 0), pltpu.roll(w, 3, 0))
            turned[f, pl.ds((HALO + LINE + k) * ROWS, ROWS)] = jnp.where(piece == PIECES - 1, seam, pltpu.roll(v, 7, 0))


def turn_out(turned, target):
    for f in range(4):
        for side in range(SIDES):
            parts = [
                turned[f, pl.ds((1 + k * ROWS) * ROWS + side * PIECES + piece, ROWS, stride=ROWS)]
                for piece in range(PIECES)
                for k in range(LINE // ROWS)
            ]
            target(f, side, jnp.concatenate(parts, axis=0).T)


def column_sweep(source, target, turned, swept, ratio):
    turn_in(source, turned)

    def some(part, last):
        at = pl.multiple_of(part * (FACES * ROWS), ROWS)
        cells = [
            turned[f, pl.ds(at, (FACES + 5) * ROWS)].reshape(FACES + 5, ROWS, LANES) for f in range(4)
        ]
        sides = [edges(c) for c in cells]
        flux = fluxes([s[0] for s in sides], [s[1] for s in sides], ratio)
        change = [now - jnp.concatenate([old, now[:-1]], axis=0) for now, old in zip(flux, last)]
        for f, value in enumerate(updated([c[2:-3] for c in cells], change)):
            swept[f, pl.ds(at, FACES * ROWS)] = value.reshape(FACES * ROWS, LANES)
        return tuple(now[-1:] for now in flux)

    none = jnp.zeros((1, ROWS, LANES), jnp.float32)
    lax.fori_loop(0, (LINE + 1) // FACES, some, (none,) * 4)
    turn_out(swept, target)


def half(ref, *index):
    return lambda f, side: ref[(f, *index, pl.ds(side * LANES, LANES))]


def into(ref, *index):
    def put(f, side, value):
        ref[(f, *index, pl.ds(side * LANES, LANES))] = value

    return put


def line(quarter, row):
    return pl.ds(quarter * (QUARTER * ROWS) + row, QUARTER, stride=ROWS)


def kernel(
    density, velocity, pressure, done, left,
    start, first, outer, turned, swept, to_up, to_down, from_up, from_down,
    in_sem, send_sem, recv_sem, ready_sem,
):
    slab = lax.axis_index("slab")
    me = lax.axis_index("pencil")
    count = lax.axis_size("pencil")
    up = lax.rem(me + 1, count)
    down = lax.rem(me + count - 1, count)
    planes = start.shape[1]
    quarters = start.shape[2] // (QUARTER * ROWS)

    place = lax.rem(me, GROUP)
    barrier = pltpu.get_barrier_semaphore()
    pl.semaphore_signal(barrier, inc=1, device_id=(slab, down), device_id_type=MESH)

    @pl.when(place < GROUP - 1)
    def _():
        pl.semaphore_signal(barrier, inc=1, device_id=(slab, up), device_id_type=MESH)

    def load(plane, f):
        source = (density.at[plane], velocity.at[0, plane], velocity.at[1, plane], pressure.at[plane])[f]
        return pltpu.make_async_copy(source, start.at[f, plane], in_sem.at[f, plane])

    for plane in range(planes):
        for f in range(4):
            load(plane, f).start()

    def copy_up(unit, n):
        part = pl.ds(unit, n)
        return pltpu.make_async_remote_copy(
            to_up.at[part], from_down.at[part], send_sem.at[0, unit], recv_sem.at[0, unit],
            device_id=(slab, up), device_id_type=MESH,
        )

    def copy_down(unit, n):
        part = pl.ds(unit, n)
        return pltpu.make_async_remote_copy(
            to_down.at[part], from_up.at[part], send_sem.at[1, unit], recv_sem.at[1, unit],
            device_id=(slab, down), device_id_type=MESH,
        )

    def messages(plane, act):
        @pl.when(plane < planes - 1)
        def _():
            for quarter in range(0, quarters, 2):
                act(plane * quarters + quarter, 2)

        @pl.when(plane == planes - 1)
        def _():
            for quarter in range(quarters):
                act(plane * quarters + quarter, 1)

    def pack(ref, plane):
        for quarter in range(quarters):
            unit = plane * quarters + quarter
            for f in range(4):
                for row in range(HALO):
                    to_up[unit, f * HALO + row] = ref[f, plane, line(quarter, ROWS - HALO + row)]
                    to_down[unit, f * HALO + row] = ref[f, plane, line(quarter, row)]

    def send(copy, plane):
        messages(plane, lambda unit, n: copy(unit, n).start())

    for f in range(4):
        load(0, f).wait()
    pack(start, 0)

    @pl.when(place == 0)
    def _():
        pl.semaphore_wait(barrier, 1)

    @pl.when(place > 0)
    def _():
        pl.semaphore_wait(barrier, 2)

    @pl.when(place == GROUP - 1)
    def _():
        pl.semaphore_signal(ready_sem, inc=1, device_id=(slab, up), device_id_type=MESH)

    send(copy_up, 0)

    @pl.when(place > 0)
    def _():
        send(copy_down, 0)

    def first_sweep(step, carry):
        plane = jnp.where(step < 2, 1 - step, step)

        @pl.when(plane > 0)
        def _():
            for f in range(4):
                load(plane, f).wait()

        column_sweep(half(start, plane), into(first, plane), turned, swept, 0.025)

        @pl.when(plane > 0)
        def _():
            pack(first, plane)
            send(copy_up, plane)

        @pl.when(jnp.logical_and(plane == 0, place == 0))
        def _():
            pl.semaphore_wait(ready_sem, 1)
            send(copy_down, 0)

        @pl.when(step > 1)
        def _():
            send(copy_down, step - 1)

        @pl.when(step == planes - 1)
        def _():
            send(copy_down, step)

        return carry

    lax.fori_loop(0, planes, first_sweep, 0)

    def arrive(unit, n):
        copy_up(unit, n).wait_recv()
        copy_down(unit, n).wait_recv()

    def outer_sweep():
        messages(0, arrive)
        for quarter in range(quarters):
            for f in range(4):
                for row in range(HALO):
                    outer[f, line(quarter, row)] = from_down[quarter, f * HALO + row]
                    outer[f, line(quarter, HALO + row)] = from_up[quarter, f * HALO + row]
                for row in range(2 * HALO, ROWS):
                    outer[f, line(quarter, row)] = from_down[quarter, f * HALO]
        column_sweep(half(outer), into(outer), turned, swept, 0.025)
        for quarter in range(quarters):
            for f in range(4):
                for row in range(HALO):
                    from_down[quarter, f * HALO + row] = outer[f, line(quarter, row)]
                    from_up[quarter, f * HALO + row] = outer[f, line(quarter, HALO + row)]

    def row_sweep(plane, quarter):
        unit = plane * quarters + quarter

        @pl.when(jnp.logical_and(jnp.logical_and(plane > 0, plane < planes - 1), lax.rem(quarter, 2) == 0))
        def _():
            arrive(unit, 2)

        @pl.when(plane == planes - 1)
        def _():
            arrive(unit, 1)

        sides, cells = [], []
        for f in (0, 2, 1, 3):
            own = [first[f, plane, line(quarter, row)][None] for row in range(ROWS)]
            below = from_down[unit, pl.ds(f * HALO, HALO)]
            above = from_up[unit, pl.ds(f * HALO, HALO)]
            sides.append(edges(jnp.concatenate([below, *own, above], axis=0)))
            cells.append(jnp.concatenate(own, axis=0))
        flux = fluxes([s[0] for s in sides], [s[1] for s in sides], 0.05)
        new = updated(cells, [now[1:] - now[:-1] for now in flux])
        for f, value in zip((0, 2, 1, 3), new):
            for row in range(ROWS):
                left[f, line(quarter, row)] = value[row]

    def later(plane, carry):
        pl.when(plane == 0)(outer_sweep)

        def row_sweeps(quarter, inner):
            row_sweep(plane, quarter)
            return inner

        lax.fori_loop(0, quarters, row_sweeps, 0)

        @pl.when(plane < planes - 1)
        def _():
            column_sweep(half(left), into(done, plane), turned, swept, 0.025)

        return carry

    lax.fori_loop(0, planes, later, 0)
    def sent(unit, n):
        copy_up(unit, n).wait_send()
        copy_down(unit, n).wait_send()

    for plane in range(planes):
        messages(plane, sent)


def last_kernel(done, left, new_density, new_velocity, new_pressure, final, turned, swept, out_sem):
    before = done.shape[1]

    def store(plane, f):
        target = (
            new_density.at[plane], new_velocity.at[0, plane], new_velocity.at[1, plane], new_pressure.at[plane],
        )[f]
        source = final.at[f] if plane == before else done.at[f, plane]
        return pltpu.make_async_copy(source, target, out_sem.at[f, plane])

    for plane in range(before):
        for f in range(4):
            store(plane, f).start()
    column_sweep(half(left), into(final), turned, swept, 0.025)
    for f in range(4):
        store(before, f).start()
    for plane in range(before + 1):
        for f in range(4):
            store(plane, f).wait()


def on_device(density, velocity, pressure):
    planes, rows, columns = density.shape
    blocks = columns // LANES
    units = planes * blocks // QUARTER

    def blocked(a):
        lead = a.shape[:-2]
        a = jnp.swapaxes(a.reshape(*lead, rows, blocks, LANES), -3, -2).reshape(*lead, blocks * rows, LANES)
        return pltpu.with_memory_space_constraint(a, pltpu.HBM)

    def unblocked(a):
        lead = a.shape[:-2]
        return jnp.swapaxes(a.reshape(*lead, blocks, rows, LANES), -3, -2).reshape(*lead, rows, columns)

    hbm = pl.BlockSpec(memory_space=pltpu.HBM)
    vmem = pl.BlockSpec(memory_space=pltpu.VMEM)
    plane = (blocks * rows, LANES)
    f32 = jnp.float32
    halo = (units, 4 * HALO, QUARTER, LANES)
    work = [
        pltpu.VMEM((4, (LINE + 2 * HALO) * ROWS, LANES), f32),
        pltpu.VMEM((4, (LINE + 1) * ROWS, LANES), f32),
    ]
    done, left = pl.pallas_call(
        kernel,
        out_shape=(pltpu.VMEM((4, planes - 1, *plane), f32), pltpu.VMEM((4, *plane), f32)),
        in_specs=[hbm] * 3,
        out_specs=(vmem, vmem),
        scratch_shapes=[
            pltpu.VMEM((4, planes, *plane), f32),
            pltpu.VMEM((4, planes, *plane), f32),
            pltpu.VMEM((4, *plane), f32),
            *work,
            pltpu.VMEM(halo, f32),
            pltpu.VMEM(halo, f32),
            pltpu.VMEM(halo, f32),
            pltpu.VMEM(halo, f32),
            pltpu.SemaphoreType.DMA((4, planes)),
            pltpu.SemaphoreType.DMA((2, units)),
            pltpu.SemaphoreType.DMA((2, units)),
            pltpu.SemaphoreType.REGULAR,
        ],
        compiler_params=pltpu.CompilerParams(
            collective_id=0, has_side_effects=True, vmem_limit_bytes=32 * 2**20
        ),
    )(blocked(density), blocked(velocity), blocked(pressure))
    outs = pl.pallas_call(
        last_kernel,
        out_shape=(pltpu.HBM((planes, *plane), f32), pltpu.HBM((2, planes, *plane), f32), pltpu.HBM((planes, *plane), f32)),
        in_specs=[vmem] * 2,
        out_specs=(hbm,) * 3,
        scratch_shapes=[pltpu.VMEM((4, *plane), f32), *work, pltpu.SemaphoreType.DMA((4, planes))],
        compiler_params=pltpu.CompilerParams(vmem_limit_bytes=16 * 2**20),
    )(*(pltpu.with_memory_space_constraint(a, pltpu.VMEM) for a in (done, left)))
    return tuple(unblocked(a) for a in outs)


def solution(mesh):
    one = P("slab", "pencil", None)
    two = P(None, "slab", "pencil", None)
    return jax.shard_map(on_device, mesh=mesh, in_specs=(one, two, one), out_specs=(one, two, one), check_vma=False)
```

```python
import jax
import jax.numpy as jnp
from jax import lax
from jax.experimental import pallas as pl
from jax.experimental.pallas import tpu as pltpu
from jax.sharding import PartitionSpec as P

MESH = pl.DeviceIdType.MESH
NEWTON = 4
LANES = 128
ROWS = 8
QUARTER = 8
HALO = 3
GROUP = 8
LINE = 32
PIECES = LANES // LINE
SIDES = 2
HALF_LINE = 16
LEAD = 4
FACES = 11


def inverse(value):
    return pl.reciprocal(value, approx=False)


def edges(values):
    d = values[1:] - values[:-1]
    here = d[1:-1]
    size = jnp.abs(here)
    sign = jnp.where(here >= 0.0, 1.0, -1.0)
    raw = 0.5 * size + sign * ((d[:-2] - d[2:]) * (1.0 / 12.0))
    to_face = jnp.minimum(jnp.maximum(raw, 0.0), size)
    beyond = size - to_face
    cells = values[2:-2]
    left = cells + sign[1:] * jnp.minimum(to_face[1:], 2.0 * beyond[:-1])
    right = cells - sign[:-1] * jnp.minimum(beyond[:-1], 2.0 * to_face[1:])
    return left[:-1], right[1:]


def fluxes(left, right, ratio):
    rho_l, un_l, ut_l, p_l = left
    rho_r, un_r, ut_r, p_r = right
    a_l = 1.2 * rho_l
    a_r = 1.2 * rho_r
    cc_l = (1.4 * rho_l) * p_l
    cc_r = (1.4 * rho_r) * p_r
    h_l = 0.5 * cc_l
    h_r = 0.5 * cc_r
    du = un_l - un_r
    dp = p_l - p_r
    inv_l = lax.rsqrt(cc_l)
    inv_r = lax.rsqrt(cc_r)
    e_r = cc_r + a_r * dp
    floor_y = 0.1 * jnp.minimum(p_l, p_r) - p_l
    y = (du - dp * inv_r) * inverse(inv_l + inv_r)
    y = jnp.maximum(y, floor_y)
    for _ in range(NEWTON):
        s_l = lax.rsqrt(a_l * y + cc_l)
        s_r = lax.rsqrt(a_r * y + e_r)
        slope = s_l * (0.5 + h_l * (s_l * s_l)) + s_r * (0.5 + h_r * (s_r * s_r))
        gap = y * s_l + ((y + dp) * s_r - du)
        y = jnp.maximum(y - gap * inverse(slope), floor_y)
    s_l = lax.rsqrt(a_l * y + cc_l)
    s_r = lax.rsqrt(a_r * y + e_r)
    pstar = y + p_l
    ustar = 0.5 * ((un_l + un_r) + ((y + dp) * s_r - y * s_l))
    from_left = ustar >= 0.0
    rho = jnp.where(from_left, rho_l, rho_r)
    un = jnp.where(from_left, un_l, un_r)
    ut = jnp.where(from_left, ut_l, ut_r)
    p = jnp.where(from_left, p_l, p_r)
    u_r = ratio * ustar
    mass = u_r * rho
    normal = mass * ustar + ratio * pstar
    trans = mass * ut
    energy = u_r * (2.5 * p + pstar) + (0.5 * mass) * (un * un + ut * ut)
    return mass, normal, trans, energy


def updated(cells, change):
    rho, un, ut, p = cells
    mass, normal, trans, lost = change
    mn = rho * un
    mt = rho * ut
    energy = 2.5 * p + 0.5 * (mn * un + mt * ut)
    rho = rho - mass
    mn = mn - normal
    mt = mt - trans
    energy = energy - lost
    inv = inverse(rho)
    un = mn * inv
    ut = mt * inv
    return rho, un, ut, 0.4 * energy - 0.2 * (mn * un + mt * ut)


def turn_in(source, turned):
    for f in range(4):
        for side in range(SIDES):
            across = source(f, side).T
            for piece in range(PIECES):
                for k in range(LINE // ROWS):
                    at = piece * LINE + k * ROWS
                    turned[f, pl.ds((HALO + k * ROWS) * ROWS + side * PIECES + piece, ROWS, stride=ROWS)] = across[at : at + ROWS]
    shape = (ROWS, LANES)
    row = lax.broadcasted_iota(jnp.int32, shape, 0)
    piece = row & (PIECES - 1)
    lane = lax.broadcasted_iota(jnp.int32, shape, 1)
    for f in range(4):
        for k in range(HALO):
            v = turned[f, pl.ds((LINE + k) * ROWS, ROWS)]
            w = pltpu.roll(v, ROWS, 1)
            seam = jnp.where(lane < ROWS, pltpu.roll(w, 1, 0), pltpu.roll(w, 5, 0))
            turned[f, pl.ds(k * ROWS, ROWS)] = jnp.where(piece == 0, seam, pltpu.roll(v, 1, 0))
            v = turned[f, pl.ds((HALO + k) * ROWS, ROWS)]
            w = pltpu.roll(v, LANES - ROWS, 1)
            seam = jnp.where(lane >= LANES - ROWS, pltpu.roll(w, 7, 0), pltpu.roll(w, 3, 0))
            turned[f, pl.ds((HALO + LINE + k) * ROWS, ROWS)] = jnp.where(piece == PIECES - 1, seam, pltpu.roll(v, 7, 0))


def turn_half(source, beyond, turned):
    edge = jnp.concatenate([rows for f in range(4) for rows in beyond(f)] * 2, axis=0).T
    row = lax.broadcasted_iota(jnp.int32, (ROWS, LANES), 0)
    lane = lax.broadcasted_iota(jnp.int32, (ROWS, LANES), 1)
    pieces = LANES // HALF_LINE
    for f in range(4):
        across = source(f).T
        for piece in range(pieces):
            for k in range(HALF_LINE // ROWS):
                at = piece * HALF_LINE + k * ROWS
                turned[f, pl.ds((HALO + k * ROWS) * ROWS + piece, ROWS, stride=ROWS)] = across[at : at + ROWS]
        before = pltpu.roll(edge[LANES - ROWS :], (LANES - 2 * ROWS * f) % LANES, 1)
        before = jnp.where(lane < ROWS, before, pltpu.roll(across[LANES - ROWS :], ROWS, 1))
        after = pltpu.roll(edge[:ROWS], LANES - 2 * ROWS * (f + 1), 1)
        after = jnp.where(lane >= LANES - ROWS, after, pltpu.roll(across[:ROWS], LANES - ROWS, 1))
        for k in range(HALO):
            v = turned[f, pl.ds((HALF_LINE + k) * ROWS, ROWS)]
            first = jnp.broadcast_to(before[ROWS - HALO + k : ROWS - HALO + k + 1], (ROWS, LANES))
            turned[f, pl.ds(k * ROWS, ROWS)] = jnp.where(row == 0, first, pltpu.roll(v, 1, 0))
            v = turned[f, pl.ds((HALO + k) * ROWS, ROWS)]
            last = jnp.broadcast_to(after[k : k + 1], (ROWS, LANES))
            turned[f, pl.ds((HALO + HALF_LINE + k) * ROWS, ROWS)] = jnp.where(row == ROWS - 1, last, pltpu.roll(v, ROWS - 1, 0))


def turn_out(turned, f, line_columns, first):
    parts = [
        turned[f, pl.ds((1 + k * ROWS) * ROWS + first + piece, ROWS, stride=ROWS)]
        for piece in range(LANES // line_columns)
        for k in range(line_columns // ROWS)
    ]
    return jnp.concatenate(parts, axis=0).T


def turned_sweep(turned, swept, ratio, faces, steps):
    def some(part, last):
        at = pl.multiple_of(part * (faces * ROWS), ROWS)
        cells = [
            turned[f, pl.ds(at, (faces + 5) * ROWS)].reshape(faces + 5, ROWS, LANES) for f in range(4)
        ]
        sides = [edges(c) for c in cells]
        flux = fluxes([s[0] for s in sides], [s[1] for s in sides], ratio)
        change = [now - jnp.concatenate([old, now[:-1]], axis=0) for now, old in zip(flux, last)]
        for f, value in enumerate(updated([c[2:-3] for c in cells], change)):
            swept[f, pl.ds(at, faces * ROWS)] = value.reshape(faces * ROWS, LANES)
        return tuple(now[-1:] for now in flux)

    none = (jnp.zeros((1, ROWS, LANES), jnp.float32),) * 4
    if steps == 1:
        some(0, none)
    else:
        lax.fori_loop(0, steps, some, none)


def column_sweep(source, target, turned, swept, ratio):
    turn_in(source, turned)
    turned_sweep(turned, swept, ratio, FACES, (LINE + 1) // FACES)
    for f in range(4):
        for side in range(SIDES):
            target(f, side, turn_out(swept, f, LINE, side * PIECES))


def half_sweep(ref, block, put, turned, swept, ratio):
    def rows(f, first, n):
        return ref[f, pl.ds(first * ROWS, n * ROWS)]

    blocks = LANES // ROWS
    turn_half(
        lambda f: rows(f, block, blocks),
        lambda f: (rows(f, block - 1, 1), rows(f, block + blocks, 1)),
        turned,
    )
    turned_sweep(turned, swept, ratio, HALF_LINE + 1, 1)
    for f in range(4):
        put(f, turn_out(swept, f, HALF_LINE, 0))


def half(ref, *index):
    return lambda f, side: ref[(f, *index, pl.ds(side * LANES, LANES))]


def into(ref, *index):
    def put(f, side, value):
        ref[(f, *index, pl.ds(side * LANES, LANES))] = value

    return put


def line(quarter, row):
    return pl.ds(quarter * (QUARTER * ROWS) + row, QUARTER, stride=ROWS)


def kernel(
    density, velocity, pressure, done, done_half, left,
    start, first, mid, outer, turned, swept, to_up, to_down, from_up, from_down,
    in_sem, send_sem, recv_sem, ready_sem,
):
    slab = lax.axis_index("slab")
    me = lax.axis_index("pencil")
    count = lax.axis_size("pencil")
    up = lax.rem(me + 1, count)
    down = lax.rem(me + count - 1, count)
    planes = start.shape[1]
    quarters = start.shape[2] // (QUARTER * ROWS)

    place = lax.rem(me, GROUP)
    barrier = pltpu.get_barrier_semaphore()
    pl.semaphore_signal(barrier, inc=1, device_id=(slab, down), device_id_type=MESH)

    @pl.when(place < GROUP - 1)
    def _():
        pl.semaphore_signal(barrier, inc=1, device_id=(slab, up), device_id_type=MESH)

    def load(plane, f):
        source = (density.at[plane], velocity.at[0, plane], velocity.at[1, plane], pressure.at[plane])[f]
        return pltpu.make_async_copy(source, start.at[f, plane], in_sem.at[f, plane])

    def load_all(plane):
        for f in range(4):
            load(plane, f).start()

    load_all(0)

    def copy_up(unit, n):
        part = pl.ds(unit, n)
        return pltpu.make_async_remote_copy(
            to_up.at[part], from_down.at[part], send_sem.at[0, unit], recv_sem.at[0, unit],
            device_id=(slab, up), device_id_type=MESH,
        )

    def copy_down(unit, n):
        part = pl.ds(unit, n)
        return pltpu.make_async_remote_copy(
            to_down.at[part], from_up.at[part], send_sem.at[1, unit], recv_sem.at[1, unit],
            device_id=(slab, down), device_id_type=MESH,
        )

    def last_order(step):
        return (step + quarters - 1) % quarters

    def messages(plane, act):
        @pl.when(plane < planes - 1)
        def _():
            for quarter in range(0, quarters, 2):
                act(plane * quarters + quarter, 2)

        @pl.when(plane == planes - 1)
        def _():
            for step in range(quarters):
                act(plane * quarters + last_order(step), 1)

    def pack(ref, plane):
        for quarter in range(quarters):
            unit = plane * quarters + quarter
            for f in range(4):
                for row in range(HALO):
                    to_up[unit, f * HALO + row] = ref[f, plane, line(quarter, ROWS - HALO + row)]
                    to_down[unit, f * HALO + row] = ref[f, plane, line(quarter, row)]

    def send(copy, plane):
        messages(plane, lambda unit, n: copy(unit, n).start())

    for f in range(4):
        load(0, f).wait()
    load_all(1)
    pack(start, 0)

    @pl.when(place == 0)
    def _():
        pl.semaphore_wait(barrier, 1)

    @pl.when(place > 0)
    def _():
        pl.semaphore_wait(barrier, 2)

    @pl.when(place == GROUP - 1)
    def _():
        pl.semaphore_signal(ready_sem, inc=1, device_id=(slab, up), device_id_type=MESH)

    ahead = place == GROUP - 1

    @pl.when(ahead)
    def _():
        send(copy_down, 0)

    send(copy_up, 0)

    @pl.when(jnp.logical_and(place > 0, jnp.logical_not(ahead)))
    def _():
        send(copy_down, 0)

    for plane in range(2, planes):
        load_all(plane)

    def first_sweep(step, carry):
        plane = jnp.where(step < 2, 1 - step, step)

        @pl.when(plane > 0)
        def _():
            for f in range(4):
                load(plane, f).wait()

        column_sweep(half(start, plane), into(first, plane), turned, swept, 0.025)

        @pl.when(plane > 0)
        def _():
            pack(first, plane)

        def both(unit, n):
            copy_up(unit, n).start()
            copy_down(unit, n).start()

        held = jnp.logical_and(place == GROUP - 1, plane >= 2)

        @pl.when(jnp.logical_and(jnp.logical_and(plane > 0, place > 0), jnp.logical_not(held)))
        def _():
            messages(plane, both)

        @pl.when(held)
        def _():
            send(copy_down, plane)

        @pl.when(jnp.logical_and(plane == 1, place == 0))
        def _():
            send(copy_up, plane)

        @pl.when(jnp.logical_and(plane == 0, place == 0))
        def _():
            pl.semaphore_wait(ready_sem, 1)
            send(copy_down, 0)
            send(copy_down, 1)

        @pl.when(jnp.logical_and(plane > 1, place == 0))
        def _():
            messages(plane, both)

        return carry

    lax.fori_loop(0, planes, first_sweep, 0)

    def arrive(unit, n):
        copy_up(unit, n).wait_recv()
        copy_down(unit, n).wait_recv()

    def outer_sweep():
        messages(0, arrive)
        for quarter in range(quarters):
            for f in range(4):
                for row in range(HALO):
                    outer[f, line(quarter, row)] = from_down[quarter, f * HALO + row]
                    outer[f, line(quarter, HALO + row)] = from_up[quarter, f * HALO + row]
                for row in range(2 * HALO, ROWS):
                    outer[f, line(quarter, row)] = from_down[quarter, f * HALO]
        column_sweep(half(outer), into(outer), turned, swept, 0.025)
        for quarter in range(quarters):
            for f in range(4):
                for row in range(HALO):
                    from_down[quarter, f * HALO + row] = outer[f, line(quarter, row)]
                    from_up[quarter, f * HALO + row] = outer[f, line(quarter, HALO + row)]

    def row_sweep(plane, quarter, ref, place):
        unit = plane * quarters + quarter
        sides, cells = [], []
        for f in (0, 2, 1, 3):
            own = [first[f, plane, line(quarter, row)][None] for row in range(ROWS)]
            below = from_down[unit, pl.ds(f * HALO, HALO)]
            above = from_up[unit, pl.ds(f * HALO, HALO)]
            sides.append(edges(jnp.concatenate([below, *own, above], axis=0)))
            cells.append(jnp.concatenate(own, axis=0))
        flux = fluxes([s[0] for s in sides], [s[1] for s in sides], 0.05)
        new = updated(cells, [now[1:] - now[:-1] for now in flux])
        for f, value in zip((0, 2, 1, 3), new):
            for row in range(ROWS):
                ref[f, line(place, row)] = value[row]

    def later(plane, carry):
        pl.when(plane == 0)(outer_sweep)

        def row_sweeps(quarter, inner):
            @pl.when(jnp.logical_and(plane > 0, lax.rem(quarter, 2) == 0))
            def _():
                arrive(plane * quarters + quarter, 2)

            row_sweep(plane, quarter, mid, quarter)
            return inner

        lax.fori_loop(0, quarters, row_sweeps, 0)
        column_sweep(half(mid), into(done, plane), turned, swept, 0.025)

        @pl.when(jnp.logical_and(place == GROUP - 1, plane + 2 >= 2))
        def _():
            pl.when(plane < planes - 2)(lambda: send(copy_up, plane + 2))

        return carry

    last = planes - 1
    lax.fori_loop(0, last, later, 0)

    def put(f, value):
        done_half[f] = value

    def last_rows(step, carry):
        quarter = last_order(step)
        arrive(last * quarters + quarter, 1)
        row_sweep(last, quarter, left, step)

        @pl.when(step == 0)
        def _():
            for f in range(4):
                left[f, pl.ds(quarters * QUARTER * ROWS, QUARTER * ROWS)] = left[f, pl.ds(0, QUARTER * ROWS)]

        @pl.when(step == quarters - 2)
        def _():
            half_sweep(left, LEAD, put, turned, swept, 0.025)

        return carry

    lax.fori_loop(0, quarters, last_rows, 0)

    def sent(unit, n):
        copy_up(unit, n).wait_send()
        copy_down(unit, n).wait_send()

    for plane in range(planes):
        messages(plane, sent)


def last_kernel(done, done_half, left, new_density, new_velocity, new_pressure, final, turned, swept, out_sem, half_sem):
    planes = done.shape[1]
    total = done.shape[2]
    size = final.shape[1]

    def target(plane, f, first, n):
        part = pl.ds(first, n)
        return (
            new_density.at[plane, part], new_velocity.at[0, plane, part],
            new_velocity.at[1, plane, part], new_pressure.at[plane, part],
        )[f]

    def store(plane, f):
        return pltpu.make_async_copy(done.at[f, plane], target(plane, f, 0, total), out_sem.at[f, plane])

    wrap = LEAD * ROWS

    def store_half(f, part):
        source, first, n = (
            (done_half.at[f, pl.ds(0, wrap)], total - wrap, wrap),
            (done_half.at[f, pl.ds(wrap, size - wrap)], 0, size - wrap),
            (final.at[f], size - wrap, size),
        )[part]
        return pltpu.make_async_copy(source, target(planes, f, first, n), half_sem.at[f, part])

    for f in range(4):
        for plane in range(planes):
            store(plane, f).start()
        store_half(f, 0).start()
        store_half(f, 1).start()

    def put(f, value):
        final[f] = value
        store_half(f, 2).start()

    half_sweep(left, LEAD + LANES // ROWS, put, turned, swept, 0.025)
    for f in range(4):
        for plane in range(planes):
            store(plane, f).wait()
        for part in range(3):
            store_half(f, part).wait()


def on_device(density, velocity, pressure):
    planes, rows, columns = density.shape
    blocks = columns // LANES
    units = planes * blocks // QUARTER

    def blocked(a):
        lead = a.shape[:-2]
        a = jnp.swapaxes(a.reshape(*lead, rows, blocks, LANES), -3, -2).reshape(*lead, blocks * rows, LANES)
        return pltpu.with_memory_space_constraint(a, pltpu.HBM)

    def unblocked(a):
        lead = a.shape[:-2]
        return jnp.swapaxes(a.reshape(*lead, blocks, rows, LANES), -3, -2).reshape(*lead, rows, columns)

    hbm = pl.BlockSpec(memory_space=pltpu.HBM)
    vmem = pl.BlockSpec(memory_space=pltpu.VMEM)
    plane = (blocks * rows, LANES)
    f32 = jnp.float32
    halo = (units, 4 * HALO, QUARTER, LANES)
    half_plane = (4, LANES, LANES)
    work = [
        pltpu.VMEM((4, (LINE + 2 * HALO) * ROWS, LANES), f32),
        pltpu.VMEM((4, (LINE + 1) * ROWS, LANES), f32),
    ]
    middle = pl.pallas_call(
        kernel,
        out_shape=(
            pltpu.VMEM((4, planes - 1, *plane), f32),
            pltpu.VMEM(half_plane, f32),
            pltpu.VMEM((4, (blocks + QUARTER) * rows, LANES), f32),
        ),
        in_specs=[hbm] * 3,
        out_specs=(vmem,) * 3,
        scratch_shapes=[
            pltpu.VMEM((4, planes, *plane), f32),
            pltpu.VMEM((4, planes, *plane), f32),
            pltpu.VMEM((4, *plane), f32),
            pltpu.VMEM((4, *plane), f32),
            *work,
            pltpu.VMEM(halo, f32),
            pltpu.VMEM(halo, f32),
            pltpu.VMEM(halo, f32),
            pltpu.VMEM(halo, f32),
            pltpu.SemaphoreType.DMA((4, planes)),
            pltpu.SemaphoreType.DMA((2, units)),
            pltpu.SemaphoreType.DMA((2, units)),
            pltpu.SemaphoreType.REGULAR,
        ],
        compiler_params=pltpu.CompilerParams(
            collective_id=0, has_side_effects=True, vmem_limit_bytes=32 * 2**20
        ),
    )(blocked(density), blocked(velocity), blocked(pressure))
    outs = pl.pallas_call(
        last_kernel,
        out_shape=(pltpu.HBM((planes, *plane), f32), pltpu.HBM((2, planes, *plane), f32), pltpu.HBM((planes, *plane), f32)),
        in_specs=[vmem] * 3,
        out_specs=(hbm,) * 3,
        scratch_shapes=[
            pltpu.VMEM(half_plane, f32),
            *work,
            pltpu.SemaphoreType.DMA((4, planes - 1)),
            pltpu.SemaphoreType.DMA((4, 3)),
        ],
        compiler_params=pltpu.CompilerParams(vmem_limit_bytes=16 * 2**20),
    )(*(pltpu.with_memory_space_constraint(a, pltpu.VMEM) for a in middle))
    return tuple(unblocked(a) for a in outs)


def solution(mesh):
    one = P("slab", "pencil", None)
    two = P(None, "slab", "pencil", None)
    return jax.shard_map(on_device, mesh=mesh, in_specs=(one, two, one), out_specs=(one, two, one), check_vma=False)
```

```python
import jax
import jax.numpy as jnp
from jax import lax
from jax.experimental import pallas as pl
from jax.experimental.pallas import tpu as pltpu
from jax.sharding import PartitionSpec as P

MESH = pl.DeviceIdType.MESH
NEWTON = 4
LANES = 128
ROWS = 8
QUARTER = 8
HALO = 3
GROUP = 8
LINE = 32
PIECES = LANES // LINE
SIDES = 2
HALF_LINE = 16
LEAD = 4
FACES = 11


def inverse(value):
    return pl.reciprocal(value, approx=False)


def edges(values):
    d = values[1:] - values[:-1]
    here = d[1:-1]
    size = jnp.abs(here)
    sign = jnp.where(here >= 0.0, 1.0, -1.0)
    raw = 0.5 * size + sign * ((d[:-2] - d[2:]) * (1.0 / 12.0))
    to_face = jnp.minimum(jnp.maximum(raw, 0.0), size)
    beyond = size - to_face
    cells = values[2:-2]
    left = cells + sign[1:] * jnp.minimum(to_face[1:], 2.0 * beyond[:-1])
    right = cells - sign[:-1] * jnp.minimum(beyond[:-1], 2.0 * to_face[1:])
    return left[:-1], right[1:]


def fluxes(left, right, ratio):
    rho_l, un_l, ut_l, p_l = left
    rho_r, un_r, ut_r, p_r = right
    a_l = 1.2 * rho_l
    a_r = 1.2 * rho_r
    cc_l = (1.4 * rho_l) * p_l
    cc_r = (1.4 * rho_r) * p_r
    h_l = 0.5 * cc_l
    h_r = 0.5 * cc_r
    du = un_l - un_r
    dp = p_l - p_r
    inv_l = lax.rsqrt(cc_l)
    inv_r = lax.rsqrt(cc_r)
    e_r = cc_r + a_r * dp
    floor_y = 0.1 * jnp.minimum(p_l, p_r) - p_l
    y = (du - dp * inv_r) * inverse(inv_l + inv_r)
    y = jnp.maximum(y, floor_y)
    for _ in range(NEWTON):
        s_l = lax.rsqrt(a_l * y + cc_l)
        s_r = lax.rsqrt(a_r * y + e_r)
        slope = s_l * (0.5 + h_l * (s_l * s_l)) + s_r * (0.5 + h_r * (s_r * s_r))
        gap = y * s_l + ((y + dp) * s_r - du)
        y = jnp.maximum(y - gap * inverse(slope), floor_y)
    s_l = lax.rsqrt(a_l * y + cc_l)
    s_r = lax.rsqrt(a_r * y + e_r)
    pstar = y + p_l
    ustar = 0.5 * ((un_l + un_r) + ((y + dp) * s_r - y * s_l))
    from_left = ustar >= 0.0
    rho = jnp.where(from_left, rho_l, rho_r)
    un = jnp.where(from_left, un_l, un_r)
    ut = jnp.where(from_left, ut_l, ut_r)
    p = jnp.where(from_left, p_l, p_r)
    u_r = ratio * ustar
    mass = u_r * rho
    normal = mass * ustar + ratio * pstar
    trans = mass * ut
    energy = u_r * (2.5 * p + pstar) + (0.5 * mass) * (un * un + ut * ut)
    return mass, normal, trans, energy


def updated(cells, change):
    rho, un, ut, p = cells
    mass, normal, trans, lost = change
    mn = rho * un
    mt = rho * ut
    energy = 2.5 * p + 0.5 * (mn * un + mt * ut)
    rho = rho - mass
    mn = mn - normal
    mt = mt - trans
    energy = energy - lost
    inv = inverse(rho)
    un = mn * inv
    ut = mt * inv
    return rho, un, ut, 0.4 * energy - 0.2 * (mn * un + mt * ut)


def turn_in(source, turned):
    for f in range(4):
        for side in range(SIDES):
            across = source(f, side).T
            for piece in range(PIECES):
                for k in range(LINE // ROWS):
                    at = piece * LINE + k * ROWS
                    turned[f, pl.ds((HALO + k * ROWS) * ROWS + side * PIECES + piece, ROWS, stride=ROWS)] = across[at : at + ROWS]
    shape = (ROWS, LANES)
    row = lax.broadcasted_iota(jnp.int32, shape, 0)
    piece = row & (PIECES - 1)
    lane = lax.broadcasted_iota(jnp.int32, shape, 1)
    for f in range(4):
        for k in range(HALO):
            v = turned[f, pl.ds((LINE + k) * ROWS, ROWS)]
            w = pltpu.roll(v, ROWS, 1)
            seam = jnp.where(lane < ROWS, pltpu.roll(w, 1, 0), pltpu.roll(w, 5, 0))
            turned[f, pl.ds(k * ROWS, ROWS)] = jnp.where(piece == 0, seam, pltpu.roll(v, 1, 0))
            v = turned[f, pl.ds((HALO + k) * ROWS, ROWS)]
            w = pltpu.roll(v, LANES - ROWS, 1)
            seam = jnp.where(lane >= LANES - ROWS, pltpu.roll(w, 7, 0), pltpu.roll(w, 3, 0))
            turned[f, pl.ds((HALO + LINE + k) * ROWS, ROWS)] = jnp.where(piece == PIECES - 1, seam, pltpu.roll(v, 7, 0))


def turn_half(source, beyond, turned):
    edge = jnp.concatenate([rows for f in range(4) for rows in beyond(f)] * 2, axis=0).T
    row = lax.broadcasted_iota(jnp.int32, (ROWS, LANES), 0)
    lane = lax.broadcasted_iota(jnp.int32, (ROWS, LANES), 1)
    pieces = LANES // HALF_LINE
    for f in range(4):
        across = source(f).T
        for piece in range(pieces):
            for k in range(HALF_LINE // ROWS):
                at = piece * HALF_LINE + k * ROWS
                turned[f, pl.ds((HALO + k * ROWS) * ROWS + piece, ROWS, stride=ROWS)] = across[at : at + ROWS]
        before = pltpu.roll(edge[LANES - ROWS :], (LANES - 2 * ROWS * f) % LANES, 1)
        before = jnp.where(lane < ROWS, before, pltpu.roll(across[LANES - ROWS :], ROWS, 1))
        after = pltpu.roll(edge[:ROWS], LANES - 2 * ROWS * (f + 1), 1)
        after = jnp.where(lane >= LANES - ROWS, after, pltpu.roll(across[:ROWS], LANES - ROWS, 1))
        for k in range(HALO):
            v = turned[f, pl.ds((HALF_LINE + k) * ROWS, ROWS)]
            first = jnp.broadcast_to(before[ROWS - HALO + k : ROWS - HALO + k + 1], (ROWS, LANES))
            turned[f, pl.ds(k * ROWS, ROWS)] = jnp.where(row == 0, first, pltpu.roll(v, 1, 0))
            v = turned[f, pl.ds((HALO + k) * ROWS, ROWS)]
            last = jnp.broadcast_to(after[k : k + 1], (ROWS, LANES))
            turned[f, pl.ds((HALO + HALF_LINE + k) * ROWS, ROWS)] = jnp.where(row == ROWS - 1, last, pltpu.roll(v, ROWS - 1, 0))


def turn_out(turned, f, line_columns, first):
    parts = [
        turned[f, pl.ds((1 + k * ROWS) * ROWS + first + piece, ROWS, stride=ROWS)]
        for piece in range(LANES // line_columns)
        for k in range(line_columns // ROWS)
    ]
    return jnp.concatenate(parts, axis=0).T


def turned_sweep(turned, swept, ratio, faces, steps):
    def some(part, last):
        at = pl.multiple_of(part * (faces * ROWS), ROWS)
        cells = [
            turned[f, pl.ds(at, (faces + 5) * ROWS)].reshape(faces + 5, ROWS, LANES) for f in range(4)
        ]
        sides = [edges(c) for c in cells]
        flux = fluxes([s[0] for s in sides], [s[1] for s in sides], ratio)
        change = [now - jnp.concatenate([old, now[:-1]], axis=0) for now, old in zip(flux, last)]
        for f, value in enumerate(updated([c[2:-3] for c in cells], change)):
            swept[f, pl.ds(at, faces * ROWS)] = value.reshape(faces * ROWS, LANES)
        return tuple(now[-1:] for now in flux)

    none = (jnp.zeros((1, ROWS, LANES), jnp.float32),) * 4
    if steps == 1:
        some(0, none)
    else:
        lax.fori_loop(0, steps, some, none)


def column_sweep(source, target, turned, swept, ratio):
    turn_in(source, turned)
    turned_sweep(turned, swept, ratio, FACES, (LINE + 1) // FACES)
    for f in range(4):
        for side in range(SIDES):
            target(f, side, turn_out(swept, f, LINE, side * PIECES))


def half_sweep(ref, block, put, turned, swept, ratio):
    def rows(f, first, n):
        return ref[f, pl.ds(first * ROWS, n * ROWS)]

    blocks = LANES // ROWS
    turn_half(
        lambda f: rows(f, block, blocks),
        lambda f: (rows(f, block - 1, 1), rows(f, block + blocks, 1)),
        turned,
    )
    turned_sweep(turned, swept, ratio, HALF_LINE + 1, 1)
    for f in range(4):
        put(f, turn_out(swept, f, HALF_LINE, 0))


def half(ref, *index):
    return lambda f, side: ref[(f, *index, pl.ds(side * LANES, LANES))]


def into(ref, *index):
    def put(f, side, value):
        ref[(f, *index, pl.ds(side * LANES, LANES))] = value

    return put


def line(quarter, row):
    return pl.ds(quarter * (QUARTER * ROWS) + row, QUARTER, stride=ROWS)


def kernel(
    density, velocity, pressure, done, done_half, left,
    start, first, mid, outer, turned, swept, seam, to_up, to_down, from_up, from_down,
    in_sem, send_sem, recv_sem, ready_sem,
):
    slab = lax.axis_index("slab")
    me = lax.axis_index("pencil")
    count = lax.axis_size("pencil")
    up = lax.rem(me + 1, count)
    down = lax.rem(me + count - 1, count)
    planes = start.shape[1]
    quarters = start.shape[2] // (QUARTER * ROWS)

    place = lax.rem(me, GROUP)
    barrier = pltpu.get_barrier_semaphore()
    pl.semaphore_signal(barrier, inc=1, device_id=(slab, down), device_id_type=MESH)

    @pl.when(place < GROUP - 1)
    def _():
        pl.semaphore_signal(barrier, inc=1, device_id=(slab, up), device_id_type=MESH)

    def load(plane, f):
        source = (density.at[plane], velocity.at[0, plane], velocity.at[1, plane], pressure.at[plane])[f]
        return pltpu.make_async_copy(source, start.at[f, plane], in_sem.at[f, plane])

    def load_all(plane):
        for f in range(4):
            load(plane, f).start()

    load_all(0)

    def copy_up(unit, n):
        part = pl.ds(unit, n)
        return pltpu.make_async_remote_copy(
            to_up.at[part], from_down.at[part], send_sem.at[0, unit], recv_sem.at[0, unit],
            device_id=(slab, up), device_id_type=MESH,
        )

    def copy_down(unit, n):
        part = pl.ds(unit, n)
        return pltpu.make_async_remote_copy(
            to_down.at[part], from_up.at[part], send_sem.at[1, unit], recv_sem.at[1, unit],
            device_id=(slab, down), device_id_type=MESH,
        )

    def last_order(step):
        return (step + quarters - 1) % quarters

    def messages(plane, act):
        @pl.when(plane < planes - 1)
        def _():
            for quarter in range(0, quarters, 2):
                act(plane * quarters + quarter, 2)

        @pl.when(plane == planes - 1)
        def _():
            for step in range(quarters):
                act(plane * quarters + last_order(step), 1)

    def pack(ref, plane):
        for quarter in range(quarters):
            unit = plane * quarters + quarter
            for f in range(4):
                for row in range(HALO):
                    to_up[unit, f * HALO + row] = ref[f, plane, line(quarter, ROWS - HALO + row)]
                    to_down[unit, f * HALO + row] = ref[f, plane, line(quarter, row)]

    def send(copy, plane):
        messages(plane, lambda unit, n: copy(unit, n).start())

    for f in range(4):
        load(0, f).wait()
    load_all(1)
    pack(start, 0)

    @pl.when(place == 0)
    def _():
        pl.semaphore_wait(barrier, 1)

    @pl.when(place > 0)
    def _():
        pl.semaphore_wait(barrier, 2)

    @pl.when(place == GROUP - 1)
    def _():
        pl.semaphore_signal(ready_sem, inc=1, device_id=(slab, up), device_id_type=MESH)

    ahead = place == GROUP - 1

    @pl.when(ahead)
    def _():
        send(copy_down, 0)

    send(copy_up, 0)

    @pl.when(jnp.logical_and(place > 0, jnp.logical_not(ahead)))
    def _():
        send(copy_down, 0)

    for plane in range(2, planes):
        load_all(plane)

    def first_sweep(step, carry):
        plane = jnp.where(step < 2, 1 - step, step)

        @pl.when(plane > 0)
        def _():
            for f in range(4):
                load(plane, f).wait()

        column_sweep(half(start, plane), into(first, plane), turned, swept, 0.025)

        @pl.when(plane > 0)
        def _():
            pack(first, plane)

        def both(unit, n):
            copy_up(unit, n).start()
            copy_down(unit, n).start()

        held = jnp.logical_and(place == GROUP - 1, plane >= 2)

        @pl.when(jnp.logical_and(jnp.logical_and(plane > 0, place > 0), jnp.logical_not(held)))
        def _():
            messages(plane, both)

        @pl.when(held)
        def _():
            send(copy_down, plane)

        @pl.when(jnp.logical_and(plane > 0, place == 0))
        def _():
            send(copy_up, plane)

        @pl.when(jnp.logical_and(plane == 2, place == 0))
        def _():
            pl.semaphore_wait(ready_sem, 1)
            send(copy_down, 0)
            send(copy_down, 1)

        @pl.when(jnp.logical_and(plane == 3, place == 0))
        def _():
            send(copy_down, 2)
            send(copy_down, 3)

        return carry

    lax.fori_loop(0, planes, first_sweep, 0)

    def arrive(unit, n):
        copy_up(unit, n).wait_recv()
        copy_down(unit, n).wait_recv()

    def outer_sweep():
        messages(0, arrive)
        for quarter in range(quarters):
            for f in range(4):
                for row in range(HALO):
                    outer[f, line(quarter, row)] = from_down[quarter, f * HALO + row]
                    outer[f, line(quarter, HALO + row)] = from_up[quarter, f * HALO + row]
                for row in range(2 * HALO, ROWS):
                    outer[f, line(quarter, row)] = from_down[quarter, f * HALO]
        column_sweep(half(outer), into(outer), turned, swept, 0.025)
        for quarter in range(quarters):
            for f in range(4):
                for row in range(HALO):
                    from_down[quarter, f * HALO + row] = outer[f, line(quarter, row)]
                    from_up[quarter, f * HALO + row] = outer[f, line(quarter, HALO + row)]

    low = ROWS - HALO

    def own_rows(f, plane, quarter, begin, end):
        return [first[f, plane, line(quarter, row)][None] for row in range(begin, end)]

    def finish_rows(cells, change, ref, place, begin):
        for f, value in zip((0, 2, 1, 3), updated(cells, change)):
            for row in range(value.shape[0]):
                ref[f, line(place, begin + row)] = value[row]

    def low_rows(plane, quarter, ref, place):
        unit = plane * quarters + quarter
        sides, cells = [], []
        for f in (0, 2, 1, 3):
            own = own_rows(f, plane, quarter, 0, ROWS)
            sides.append(edges(jnp.concatenate([from_down[unit, pl.ds(f * HALO, HALO)], *own], axis=0)))
            cells.append(jnp.concatenate(own[:low], axis=0))
        flux = fluxes([s[0] for s in sides], [s[1] for s in sides], 0.05)
        finish_rows(cells, [now[1:] - now[:-1] for now in flux], ref, place, 0)
        for f, now in enumerate(flux):
            seam[place, f] = now[low]

    def high_rows(plane, quarter, ref, place):
        unit = plane * quarters + quarter
        sides, cells = [], []
        for f in (0, 2, 1, 3):
            own = own_rows(f, plane, quarter, HALO, ROWS)
            sides.append(edges(jnp.concatenate([*own, from_up[unit, pl.ds(f * HALO, HALO)]], axis=0)))
            cells.append(jnp.concatenate(own[low - HALO :], axis=0))
        flux = fluxes([s[0] for s in sides], [s[1] for s in sides], 0.05)
        change = [now - jnp.concatenate([seam[place, f][None], now[:-1]], axis=0) for f, now in enumerate(flux)]
        finish_rows(cells, change, ref, place, low)

    def later(plane, carry):
        pl.when(plane == 0)(outer_sweep)

        def rows_of(part, copy):
            def one(quarter, inner):
                @pl.when(jnp.logical_and(plane > 0, lax.rem(quarter, 2) == 0))
                def _():
                    copy(plane * quarters + quarter, 2).wait_recv()

                part(plane, quarter, mid, quarter)
                return inner

            lax.fori_loop(0, quarters, one, 0)

        rows_of(low_rows, copy_up)
        rows_of(high_rows, copy_down)
        column_sweep(half(mid), into(done, plane), turned, swept, 0.025)

        @pl.when(jnp.logical_and(place == GROUP - 1, plane < planes - 2))
        def _():
            send(copy_up, plane + 2)

        return carry

    last = planes - 1
    lax.fori_loop(0, last, later, 0)

    def put(f, value):
        done_half[f] = value

    def last_low(step, carry):
        quarter = last_order(step)
        copy_up(last * quarters + quarter, 1).wait_recv()
        low_rows(last, quarter, left, step)
        return carry

    def last_high(step, carry):
        quarter = last_order(step)
        copy_down(last * quarters + quarter, 1).wait_recv()
        high_rows(last, quarter, left, step)
        return carry

    lax.fori_loop(0, quarters - 1, last_low, 0)
    lax.fori_loop(0, quarters - 1, last_high, 0)
    for f in range(4):
        left[f, pl.ds(quarters * QUARTER * ROWS, QUARTER * ROWS)] = left[f, pl.ds(0, QUARTER * ROWS)]
    last_low(quarters - 1, 0)
    half_sweep(left, LEAD, put, turned, swept, 0.025)
    last_high(quarters - 1, 0)

    def sent(unit, n):
        copy_up(unit, n).wait_send()
        copy_down(unit, n).wait_send()

    for plane in range(planes):
        messages(plane, sent)


def last_kernel(done, done_half, left, new_density, new_velocity, new_pressure, final, turned, swept, out_sem, half_sem):
    planes = done.shape[1]
    total = done.shape[2]
    size = final.shape[1]

    def target(plane, f, first, n):
        part = pl.ds(first, n)
        return (
            new_density.at[plane, part], new_velocity.at[0, plane, part],
            new_velocity.at[1, plane, part], new_pressure.at[plane, part],
        )[f]

    def store(f):
        return pltpu.make_async_copy(done.at[f], target(pl.ds(0, planes), f, 0, total), out_sem.at[f])

    wrap = LEAD * ROWS

    def store_half(f, part):
        source, first, n = (
            (done_half.at[f, pl.ds(0, wrap)], total - wrap, wrap),
            (done_half.at[f, pl.ds(wrap, size - wrap)], 0, size - wrap),
            (final.at[f], size - wrap, size),
        )[part]
        return pltpu.make_async_copy(source, target(planes, f, first, n), half_sem.at[f, part])

    for f in range(4):
        store(f).start()
        store_half(f, 0).start()
        store_half(f, 1).start()

    def put(f, value):
        final[f] = value
        store_half(f, 2).start()

    half_sweep(left, LEAD + LANES // ROWS, put, turned, swept, 0.025)
    for f in range(4):
        store(f).wait()
        for part in range(3):
            store_half(f, part).wait()


def on_device(density, velocity, pressure):
    planes, rows, columns = density.shape
    blocks = columns // LANES
    units = planes * blocks // QUARTER

    def blocked(a):
        lead = a.shape[:-2]
        a = jnp.swapaxes(a.reshape(*lead, rows, blocks, LANES), -3, -2).reshape(*lead, blocks * rows, LANES)
        return pltpu.with_memory_space_constraint(a, pltpu.HBM)

    def unblocked(a):
        lead = a.shape[:-2]
        return jnp.swapaxes(a.reshape(*lead, blocks, rows, LANES), -3, -2).reshape(*lead, rows, columns)

    hbm = pl.BlockSpec(memory_space=pltpu.HBM)
    vmem = pl.BlockSpec(memory_space=pltpu.VMEM)
    plane = (blocks * rows, LANES)
    f32 = jnp.float32
    halo = (units, 4 * HALO, QUARTER, LANES)
    half_plane = (4, LANES, LANES)
    work = [
        pltpu.VMEM((4, (LINE + 2 * HALO) * ROWS, LANES), f32),
        pltpu.VMEM((4, (LINE + 1) * ROWS, LANES), f32),
    ]
    middle = pl.pallas_call(
        kernel,
        out_shape=(
            pltpu.VMEM((4, planes - 1, *plane), f32),
            pltpu.VMEM(half_plane, f32),
            pltpu.VMEM((4, (blocks + QUARTER) * rows, LANES), f32),
        ),
        in_specs=[hbm] * 3,
        out_specs=(vmem,) * 3,
        scratch_shapes=[
            pltpu.VMEM((4, planes, *plane), f32),
            pltpu.VMEM((4, planes, *plane), f32),
            pltpu.VMEM((4, *plane), f32),
            pltpu.VMEM((4, *plane), f32),
            *work,
            pltpu.VMEM((blocks // QUARTER, 4, QUARTER, LANES), f32),
            pltpu.VMEM(halo, f32),
            pltpu.VMEM(halo, f32),
            pltpu.VMEM(halo, f32),
            pltpu.VMEM(halo, f32),
            pltpu.SemaphoreType.DMA((4, planes)),
            pltpu.SemaphoreType.DMA((2, units)),
            pltpu.SemaphoreType.DMA((2, units)),
            pltpu.SemaphoreType.REGULAR,
        ],
        compiler_params=pltpu.CompilerParams(
            collective_id=0, has_side_effects=True, vmem_limit_bytes=32 * 2**20
        ),
    )(blocked(density), blocked(velocity), blocked(pressure))
    outs = pl.pallas_call(
        last_kernel,
        out_shape=(pltpu.HBM((planes, *plane), f32), pltpu.HBM((2, planes, *plane), f32), pltpu.HBM((planes, *plane), f32)),
        in_specs=[vmem] * 3,
        out_specs=(hbm,) * 3,
        scratch_shapes=[
            pltpu.VMEM(half_plane, f32),
            *work,
            pltpu.SemaphoreType.DMA((4,)),
            pltpu.SemaphoreType.DMA((4, 3)),
        ],
        compiler_params=pltpu.CompilerParams(vmem_limit_bytes=16 * 2**20),
    )(*(pltpu.with_memory_space_constraint(a, pltpu.VMEM) for a in middle))
    return tuple(unblocked(a) for a in outs)


def solution(mesh):
    one = P("slab", "pencil", None)
    two = P(None, "slab", "pencil", None)
    return jax.shard_map(on_device, mesh=mesh, in_specs=(one, two, one), out_specs=(one, two, one), check_vma=False)
```

```python
import jax
import jax.numpy as jnp
from jax import lax
from jax.experimental import pallas as pl
from jax.experimental.pallas import tpu as pltpu
from jax.sharding import PartitionSpec as P

MESH = pl.DeviceIdType.MESH
NEWTON = 4
LANES = 128
ROWS = 8
QUARTER = 8
HALO = 3
GROUP = 8
LINE = 32
PIECES = LANES // LINE
SIDES = 2
HALF_LINE = 16
LEAD = 4
FACES = 11


def inverse(value):
    return pl.reciprocal(value, approx=False)


def edges(values):
    d = values[1:] - values[:-1]
    here = d[1:-1]
    size = jnp.abs(here)
    sign = jnp.where(here >= 0.0, 1.0, -1.0)
    raw = 0.5 * size + sign * ((d[:-2] - d[2:]) * (1.0 / 12.0))
    to_face = jnp.minimum(jnp.maximum(raw, 0.0), size)
    beyond = size - to_face
    cells = values[2:-2]
    left = cells + sign[1:] * jnp.minimum(to_face[1:], 2.0 * beyond[:-1])
    right = cells - sign[:-1] * jnp.minimum(beyond[:-1], 2.0 * to_face[1:])
    return left[:-1], right[1:]


def fluxes(left, right, ratio):
    rho_l, un_l, ut_l, p_l = left
    rho_r, un_r, ut_r, p_r = right
    a_l = 1.2 * rho_l
    a_r = 1.2 * rho_r
    cc_l = (1.4 * rho_l) * p_l
    cc_r = (1.4 * rho_r) * p_r
    h_l = 0.5 * cc_l
    h_r = 0.5 * cc_r
    du = un_l - un_r
    dp = p_l - p_r
    inv_l = lax.rsqrt(cc_l)
    inv_r = lax.rsqrt(cc_r)
    e_r = cc_r + a_r * dp
    floor_y = 0.1 * jnp.minimum(p_l, p_r) - p_l
    y = (du - dp * inv_r) * inverse(inv_l + inv_r)
    y = jnp.maximum(y, floor_y)
    for _ in range(NEWTON):
        s_l = lax.rsqrt(a_l * y + cc_l)
        s_r = lax.rsqrt(a_r * y + e_r)
        slope = s_l * (0.5 + h_l * (s_l * s_l)) + s_r * (0.5 + h_r * (s_r * s_r))
        gap = y * s_l + ((y + dp) * s_r - du)
        y = jnp.maximum(y - gap * inverse(slope), floor_y)
    s_l = lax.rsqrt(a_l * y + cc_l)
    s_r = lax.rsqrt(a_r * y + e_r)
    pstar = y + p_l
    ustar = 0.5 * ((un_l + un_r) + ((y + dp) * s_r - y * s_l))
    from_left = ustar >= 0.0
    rho = jnp.where(from_left, rho_l, rho_r)
    un = jnp.where(from_left, un_l, un_r)
    ut = jnp.where(from_left, ut_l, ut_r)
    p = jnp.where(from_left, p_l, p_r)
    u_r = ratio * ustar
    mass = u_r * rho
    normal = mass * ustar + ratio * pstar
    trans = mass * ut
    energy = u_r * (2.5 * p + pstar) + (0.5 * mass) * (un * un + ut * ut)
    return mass, normal, trans, energy


def updated(cells, change):
    rho, un, ut, p = cells
    mass, normal, trans, lost = change
    mn = rho * un
    mt = rho * ut
    energy = 2.5 * p + 0.5 * (mn * un + mt * ut)
    rho = rho - mass
    mn = mn - normal
    mt = mt - trans
    energy = energy - lost
    inv = inverse(rho)
    un = mn * inv
    ut = mt * inv
    return rho, un, ut, 0.4 * energy - 0.2 * (mn * un + mt * ut)


def turn_in(source, turned):
    for f in range(4):
        for side in range(SIDES):
            across = source(f, side).T
            for piece in range(PIECES):
                for k in range(LINE // ROWS):
                    at = piece * LINE + k * ROWS
                    turned[f, pl.ds((HALO + k * ROWS) * ROWS + side * PIECES + piece, ROWS, stride=ROWS)] = across[at : at + ROWS]
    shape = (ROWS, LANES)
    row = lax.broadcasted_iota(jnp.int32, shape, 0)
    piece = row & (PIECES - 1)
    lane = lax.broadcasted_iota(jnp.int32, shape, 1)
    for f in range(4):
        for k in range(HALO):
            v = turned[f, pl.ds((LINE + k) * ROWS, ROWS)]
            w = pltpu.roll(v, ROWS, 1)
            seam = jnp.where(lane < ROWS, pltpu.roll(w, 1, 0), pltpu.roll(w, 5, 0))
            turned[f, pl.ds(k * ROWS, ROWS)] = jnp.where(piece == 0, seam, pltpu.roll(v, 1, 0))
            v = turned[f, pl.ds((HALO + k) * ROWS, ROWS)]
            w = pltpu.roll(v, LANES - ROWS, 1)
            seam = jnp.where(lane >= LANES - ROWS, pltpu.roll(w, 7, 0), pltpu.roll(w, 3, 0))
            turned[f, pl.ds((HALO + LINE + k) * ROWS, ROWS)] = jnp.where(piece == PIECES - 1, seam, pltpu.roll(v, 7, 0))


def turn_half(source, beyond, turned):
    edge = jnp.concatenate([rows for f in range(4) for rows in beyond(f)] * 2, axis=0).T
    row = lax.broadcasted_iota(jnp.int32, (ROWS, LANES), 0)
    lane = lax.broadcasted_iota(jnp.int32, (ROWS, LANES), 1)
    pieces = LANES // HALF_LINE
    for f in range(4):
        across = source(f).T
        for piece in range(pieces):
            for k in range(HALF_LINE // ROWS):
                at = piece * HALF_LINE + k * ROWS
                turned[f, pl.ds((HALO + k * ROWS) * ROWS + piece, ROWS, stride=ROWS)] = across[at : at + ROWS]
        before = pltpu.roll(edge[LANES - ROWS :], (LANES - 2 * ROWS * f) % LANES, 1)
        before = jnp.where(lane < ROWS, before, pltpu.roll(across[LANES - ROWS :], ROWS, 1))
        after = pltpu.roll(edge[:ROWS], LANES - 2 * ROWS * (f + 1), 1)
        after = jnp.where(lane >= LANES - ROWS, after, pltpu.roll(across[:ROWS], LANES - ROWS, 1))
        for k in range(HALO):
            v = turned[f, pl.ds((HALF_LINE + k) * ROWS, ROWS)]
            first = jnp.broadcast_to(before[ROWS - HALO + k : ROWS - HALO + k + 1], (ROWS, LANES))
            turned[f, pl.ds(k * ROWS, ROWS)] = jnp.where(row == 0, first, pltpu.roll(v, 1, 0))
            v = turned[f, pl.ds((HALO + k) * ROWS, ROWS)]
            last = jnp.broadcast_to(after[k : k + 1], (ROWS, LANES))
            turned[f, pl.ds((HALO + HALF_LINE + k) * ROWS, ROWS)] = jnp.where(row == ROWS - 1, last, pltpu.roll(v, ROWS - 1, 0))


def turn_out(turned, f, line_columns, first):
    parts = [
        turned[f, pl.ds((1 + k * ROWS) * ROWS + first + piece, ROWS, stride=ROWS)]
        for piece in range(LANES // line_columns)
        for k in range(line_columns // ROWS)
    ]
    return jnp.concatenate(parts, axis=0).T


def turned_sweep(turned, swept, ratio, faces, steps):
    def some(part, last):
        at = pl.multiple_of(part * (faces * ROWS), ROWS)
        cells = [
            turned[f, pl.ds(at, (faces + 5) * ROWS)].reshape(faces + 5, ROWS, LANES) for f in range(4)
        ]
        sides = [edges(c) for c in cells]
        flux = fluxes([s[0] for s in sides], [s[1] for s in sides], ratio)
        change = [now - jnp.concatenate([old, now[:-1]], axis=0) for now, old in zip(flux, last)]
        for f, value in enumerate(updated([c[2:-3] for c in cells], change)):
            swept[f, pl.ds(at, faces * ROWS)] = value.reshape(faces * ROWS, LANES)
        return tuple(now[-1:] for now in flux)

    none = (jnp.zeros((1, ROWS, LANES), jnp.float32),) * 4
    if steps == 1:
        some(0, none)
    else:
        lax.fori_loop(0, steps, some, none)


def column_sweep(source, target, turned, swept, ratio):
    turn_in(source, turned)
    turned_sweep(turned, swept, ratio, FACES, (LINE + 1) // FACES)
    for f in range(4):
        for side in range(SIDES):
            target(f, side, turn_out(swept, f, LINE, side * PIECES))


def half_sweep(ref, block, put, turned, swept, ratio):
    def rows(f, first, n):
        return ref[f, pl.ds(first * ROWS, n * ROWS)]

    blocks = LANES // ROWS
    turn_half(
        lambda f: rows(f, block, blocks),
        lambda f: (rows(f, block - 1, 1), rows(f, block + blocks, 1)),
        turned,
    )
    turned_sweep(turned, swept, ratio, HALF_LINE + 1, 1)
    for f in range(4):
        put(f, turn_out(swept, f, HALF_LINE, 0))


def half(ref, *index):
    return lambda f, side: ref[(f, *index, pl.ds(side * LANES, LANES))]


def into(ref, *index):
    def put(f, side, value):
        ref[(f, *index, pl.ds(side * LANES, LANES))] = value

    return put


def line(quarter, row):
    return pl.ds(quarter * (QUARTER * ROWS) + row, QUARTER, stride=ROWS)


def kernel(
    density, velocity, pressure, done, done_half, left,
    start, first, mid, outer, turned, swept, seam, to_up, to_down, from_up, from_down,
    in_sem, send_sem, recv_sem, ready_sem,
):
    slab = lax.axis_index("slab")
    me = lax.axis_index("pencil")
    count = lax.axis_size("pencil")
    up = lax.rem(me + 1, count)
    down = lax.rem(me + count - 1, count)
    planes = start.shape[1]
    quarters = start.shape[2] // (QUARTER * ROWS)

    place = lax.rem(me, GROUP)
    barrier = pltpu.get_barrier_semaphore()
    pl.semaphore_signal(barrier, inc=1, device_id=(slab, down), device_id_type=MESH)

    @pl.when(place < GROUP - 1)
    def _():
        pl.semaphore_signal(barrier, inc=1, device_id=(slab, up), device_id_type=MESH)

    def load(plane, f):
        source = (density.at[plane], velocity.at[0, plane], velocity.at[1, plane], pressure.at[plane])[f]
        return pltpu.make_async_copy(source, start.at[f, plane], in_sem.at[f, plane])

    def load_all(plane):
        for f in range(4):
            load(plane, f).start()

    load_all(0)

    def copy_up(unit, n):
        part = pl.ds(unit, n)
        return pltpu.make_async_remote_copy(
            to_up.at[part], from_down.at[part], send_sem.at[0, unit], recv_sem.at[0, unit],
            device_id=(slab, up), device_id_type=MESH,
        )

    def copy_down(unit, n):
        part = pl.ds(unit, n)
        return pltpu.make_async_remote_copy(
            to_down.at[part], from_up.at[part], send_sem.at[1, unit], recv_sem.at[1, unit],
            device_id=(slab, down), device_id_type=MESH,
        )

    def last_order(step):
        return (step + quarters - 1) % quarters

    def messages(plane, act):
        @pl.when(plane < planes - 2)
        def _():
            for quarter in range(0, quarters, 2):
                act(plane * quarters + quarter, 2)

        @pl.when(jnp.logical_and(plane >= planes - 2, plane < planes - 1))
        def _():
            for quarter in range(quarters):
                act(plane * quarters + quarter, 1)

        @pl.when(plane == planes - 1)
        def _():
            for step in range(quarters):
                act(plane * quarters + last_order(step), 1)

    def pack(ref, plane):
        for quarter in range(quarters):
            unit = plane * quarters + quarter
            for f in range(4):
                for row in range(HALO):
                    to_up[unit, f * HALO + row] = ref[f, plane, line(quarter, ROWS - HALO + row)]
                    to_down[unit, f * HALO + row] = ref[f, plane, line(quarter, row)]

    def send(copy, plane):
        messages(plane, lambda unit, n: copy(unit, n).start())

    for f in range(4):
        load(0, f).wait()
    load_all(1)
    pack(start, 0)

    @pl.when(place == 0)
    def _():
        pl.semaphore_wait(barrier, 1)

    @pl.when(place > 0)
    def _():
        pl.semaphore_wait(barrier, 2)

    @pl.when(place == GROUP - 1)
    def _():
        pl.semaphore_signal(ready_sem, inc=1, device_id=(slab, up), device_id_type=MESH)

    ahead = place == GROUP - 1

    @pl.when(ahead)
    def _():
        send(copy_down, 0)

    send(copy_up, 0)

    @pl.when(jnp.logical_and(place > 0, jnp.logical_not(ahead)))
    def _():
        send(copy_down, 0)

    for plane in range(2, planes):
        load_all(plane)

    def first_sweep(step, carry):
        plane = jnp.where(step < 2, 1 - step, step)

        @pl.when(plane > 0)
        def _():
            for f in range(4):
                load(plane, f).wait()

        column_sweep(half(start, plane), into(first, plane), turned, swept, 0.025)

        @pl.when(plane > 0)
        def _():
            pack(first, plane)

        def both(unit, n):
            copy_up(unit, n).start()
            copy_down(unit, n).start()

        held = jnp.logical_and(place == GROUP - 1, plane >= 2)

        @pl.when(jnp.logical_and(jnp.logical_and(plane > 0, place > 0), jnp.logical_not(held)))
        def _():
            messages(plane, both)

        @pl.when(held)
        def _():
            send(copy_down, plane)

        @pl.when(jnp.logical_and(plane > 0, place == 0))
        def _():
            send(copy_up, plane)

        @pl.when(jnp.logical_and(plane == 2, place == 0))
        def _():
            pl.semaphore_wait(ready_sem, 1)
            send(copy_down, 0)
            send(copy_down, 1)

        @pl.when(jnp.logical_and(plane == 3, place == 0))
        def _():
            send(copy_down, 2)
            send(copy_down, 3)

        return carry

    lax.fori_loop(0, planes, first_sweep, 0)

    def arrive(unit, n):
        copy_up(unit, n).wait_recv()
        copy_down(unit, n).wait_recv()

    def outer_sweep():
        messages(0, arrive)
        for quarter in range(quarters):
            for f in range(4):
                for row in range(HALO):
                    outer[f, line(quarter, row)] = from_down[quarter, f * HALO + row]
                    outer[f, line(quarter, HALO + row)] = from_up[quarter, f * HALO + row]
                for row in range(2 * HALO, ROWS):
                    outer[f, line(quarter, row)] = from_down[quarter, f * HALO]
        column_sweep(half(outer), into(outer), turned, swept, 0.025)
        for quarter in range(quarters):
            for f in range(4):
                for row in range(HALO):
                    from_down[quarter, f * HALO + row] = outer[f, line(quarter, row)]
                    from_up[quarter, f * HALO + row] = outer[f, line(quarter, HALO + row)]

    low = ROWS - HALO

    def own_rows(f, plane, quarter, begin, end):
        return [first[f, plane, line(quarter, row)][None] for row in range(begin, end)]

    def finish_rows(cells, change, ref, place, begin):
        for f, value in zip((0, 2, 1, 3), updated(cells, change)):
            for row in range(value.shape[0]):
                ref[f, line(place, begin + row)] = value[row]

    def low_rows(plane, quarter, ref, place):
        unit = plane * quarters + quarter
        sides, cells = [], []
        for f in (0, 2, 1, 3):
            own = own_rows(f, plane, quarter, 0, ROWS)
            sides.append(edges(jnp.concatenate([from_down[unit, pl.ds(f * HALO, HALO)], *own], axis=0)))
            cells.append(jnp.concatenate(own[:low], axis=0))
        flux = fluxes([s[0] for s in sides], [s[1] for s in sides], 0.05)
        finish_rows(cells, [now[1:] - now[:-1] for now in flux], ref, place, 0)
        for f, now in enumerate(flux):
            seam[place, f] = now[low]

    def high_rows(plane, quarter, ref, place):
        unit = plane * quarters + quarter
        sides, cells = [], []
        for f in (0, 2, 1, 3):
            own = own_rows(f, plane, quarter, HALO, ROWS)
            sides.append(edges(jnp.concatenate([*own, from_up[unit, pl.ds(f * HALO, HALO)]], axis=0)))
            cells.append(jnp.concatenate(own[low - HALO :], axis=0))
        flux = fluxes([s[0] for s in sides], [s[1] for s in sides], 0.05)
        change = [now - jnp.concatenate([seam[place, f][None], now[:-1]], axis=0) for f, now in enumerate(flux)]
        finish_rows(cells, change, ref, place, low)

    def later(plane, carry):
        pl.when(plane == 0)(outer_sweep)

        def rows_of(part, copy):
            def one(quarter, inner):
                @pl.when(jnp.logical_and(jnp.logical_and(plane > 0, plane < planes - 2), lax.rem(quarter, 2) == 0))
                def _():
                    copy(plane * quarters + quarter, 2).wait_recv()

                @pl.when(plane >= planes - 2)
                def _():
                    copy(plane * quarters + quarter, 1).wait_recv()

                part(plane, quarter, mid, quarter)
                return inner

            lax.fori_loop(0, quarters, one, 0)

        rows_of(low_rows, copy_up)
        rows_of(high_rows, copy_down)
        column_sweep(half(mid), into(done, plane), turned, swept, 0.025)

        @pl.when(jnp.logical_and(place == GROUP - 1, plane < planes - 2))
        def _():
            send(copy_up, plane + 2)

        return carry

    last = planes - 1
    lax.fori_loop(0, last, later, 0)

    def put(f, value):
        done_half[f] = value

    def last_low(step, carry):
        quarter = last_order(step)
        copy_up(last * quarters + quarter, 1).wait_recv()
        low_rows(last, quarter, left, step)
        return carry

    def last_high(step, carry):
        quarter = last_order(step)
        copy_down(last * quarters + quarter, 1).wait_recv()
        high_rows(last, quarter, left, step)
        return carry

    lax.fori_loop(0, quarters - 1, last_low, 0)
    lax.fori_loop(0, quarters - 1, last_high, 0)
    for f in range(4):
        left[f, pl.ds(quarters * QUARTER * ROWS, QUARTER * ROWS)] = left[f, pl.ds(0, QUARTER * ROWS)]
    last_low(quarters - 1, 0)
    half_sweep(left, LEAD, put, turned, swept, 0.025)
    last_high(quarters - 1, 0)

    def sent(unit, n):
        copy_up(unit, n).wait_send()
        copy_down(unit, n).wait_send()

    for plane in range(planes):
        messages(plane, sent)


def last_kernel(done, done_half, left, new_density, new_velocity, new_pressure, final, turned, swept, out_sem, half_sem):
    planes = done.shape[1]
    total = done.shape[2]
    size = final.shape[1]

    def target(plane, f, first, n):
        part = pl.ds(first, n)
        return (
            new_density.at[plane, part], new_velocity.at[0, plane, part],
            new_velocity.at[1, plane, part], new_pressure.at[plane, part],
        )[f]

    def store(f):
        return pltpu.make_async_copy(done.at[f], target(pl.ds(0, planes), f, 0, total), out_sem.at[f])

    wrap = LEAD * ROWS

    def store_half(f, part):
        source, first, n = (
            (done_half.at[f, pl.ds(0, wrap)], total - wrap, wrap),
            (done_half.at[f, pl.ds(wrap, size - wrap)], 0, size - wrap),
            (final.at[f], size - wrap, size),
        )[part]
        return pltpu.make_async_copy(source, target(planes, f, first, n), half_sem.at[f, part])

    for f in range(4):
        store(f).start()
        store_half(f, 0).start()
        store_half(f, 1).start()

    def put(f, value):
        final[f] = value
        store_half(f, 2).start()

    half_sweep(left, LEAD + LANES // ROWS, put, turned, swept, 0.025)
    for f in range(4):
        store(f).wait()
        for part in range(3):
            store_half(f, part).wait()


def on_device(density, velocity, pressure):
    planes, rows, columns = density.shape
    blocks = columns // LANES
    units = planes * blocks // QUARTER

    def blocked(a):
        lead = a.shape[:-2]
        a = jnp.swapaxes(a.reshape(*lead, rows, blocks, LANES), -3, -2).reshape(*lead, blocks * rows, LANES)
        return pltpu.with_memory_space_constraint(a, pltpu.HBM)

    def unblocked(a):
        lead = a.shape[:-2]
        return jnp.swapaxes(a.reshape(*lead, blocks, rows, LANES), -3, -2).reshape(*lead, rows, columns)

    hbm = pl.BlockSpec(memory_space=pltpu.HBM)
    vmem = pl.BlockSpec(memory_space=pltpu.VMEM)
    plane = (blocks * rows, LANES)
    f32 = jnp.float32
    halo = (units, 4 * HALO, QUARTER, LANES)
    half_plane = (4, LANES, LANES)
    work = [
        pltpu.VMEM((4, (LINE + 2 * HALO) * ROWS, LANES), f32),
        pltpu.VMEM((4, (LINE + 1) * ROWS, LANES), f32),
    ]
    middle = pl.pallas_call(
        kernel,
        out_shape=(
            pltpu.VMEM((4, planes - 1, *plane), f32),
            pltpu.VMEM(half_plane, f32),
            pltpu.VMEM((4, (blocks + QUARTER) * rows, LANES), f32),
        ),
        in_specs=[hbm] * 3,
        out_specs=(vmem,) * 3,
        scratch_shapes=[
            pltpu.VMEM((4, planes, *plane), f32),
            pltpu.VMEM((4, planes, *plane), f32),
            pltpu.VMEM((4, *plane), f32),
            pltpu.VMEM((4, *plane), f32),
            *work,
            pltpu.VMEM((blocks // QUARTER, 4, QUARTER, LANES), f32),
            pltpu.VMEM(halo, f32),
            pltpu.VMEM(halo, f32),
            pltpu.VMEM(halo, f32),
            pltpu.VMEM(halo, f32),
            pltpu.SemaphoreType.DMA((4, planes)),
            pltpu.SemaphoreType.DMA((2, units)),
            pltpu.SemaphoreType.DMA((2, units)),
            pltpu.SemaphoreType.REGULAR,
        ],
        compiler_params=pltpu.CompilerParams(
            collective_id=0, has_side_effects=True, vmem_limit_bytes=32 * 2**20
        ),
    )(blocked(density), blocked(velocity), blocked(pressure))
    outs = pl.pallas_call(
        last_kernel,
        out_shape=(pltpu.HBM((planes, *plane), f32), pltpu.HBM((2, planes, *plane), f32), pltpu.HBM((planes, *plane), f32)),
        in_specs=[vmem] * 3,
        out_specs=(hbm,) * 3,
        scratch_shapes=[
            pltpu.VMEM(half_plane, f32),
            *work,
            pltpu.SemaphoreType.DMA((4,)),
            pltpu.SemaphoreType.DMA((4, 3)),
        ],
        compiler_params=pltpu.CompilerParams(vmem_limit_bytes=16 * 2**20),
    )(*(pltpu.with_memory_space_constraint(a, pltpu.VMEM) for a in middle))
    return tuple(unblocked(a) for a in outs)


def solution(mesh):
    one = P("slab", "pencil", None)
    two = P(None, "slab", "pencil", None)
    return jax.shard_map(on_device, mesh=mesh, in_specs=(one, two, one), out_specs=(one, two, one), check_vma=False)
```

```python
import jax
import jax.numpy as jnp
from jax import lax
from jax.experimental import pallas as pl
from jax.experimental.pallas import tpu as pltpu
from jax.sharding import PartitionSpec as P

MESH = pl.DeviceIdType.MESH
NEWTON = 4
LANES = 128
ROWS = 8
QUARTER = 8
HALO = 3
GROUP = 8
LINE = 32
PIECES = LANES // LINE
SIDES = 2
HALF_LINE = 16
LEAD = 4
FACES = 11


def inverse(value):
    return pl.reciprocal(value, approx=False)


def edges(values):
    d = values[1:] - values[:-1]
    here = d[1:-1]
    size = jnp.abs(here)
    sign = jnp.where(here >= 0.0, 1.0, -1.0)
    raw = 0.5 * size + sign * ((d[:-2] - d[2:]) * (1.0 / 12.0))
    to_face = jnp.minimum(jnp.maximum(raw, 0.0), size)
    beyond = size - to_face
    cells = values[2:-2]
    left = cells + sign[1:] * jnp.minimum(to_face[1:], 2.0 * beyond[:-1])
    right = cells - sign[:-1] * jnp.minimum(beyond[:-1], 2.0 * to_face[1:])
    return left[:-1], right[1:]


def fluxes(left, right, ratio):
    rho_l, un_l, ut_l, p_l = left
    rho_r, un_r, ut_r, p_r = right
    a_l = 1.2 * rho_l
    a_r = 1.2 * rho_r
    cc_l = (1.4 * rho_l) * p_l
    cc_r = (1.4 * rho_r) * p_r
    h_l = 0.5 * cc_l
    h_r = 0.5 * cc_r
    du = un_l - un_r
    dp = p_l - p_r
    inv_l = lax.rsqrt(cc_l)
    inv_r = lax.rsqrt(cc_r)
    e_r = cc_r + a_r * dp
    floor_y = 0.1 * jnp.minimum(p_l, p_r) - p_l
    y = (du - dp * inv_r) * inverse(inv_l + inv_r)
    y = jnp.maximum(y, floor_y)
    for _ in range(NEWTON):
        s_l = lax.rsqrt(a_l * y + cc_l)
        s_r = lax.rsqrt(a_r * y + e_r)
        slope = s_l * (0.5 + h_l * (s_l * s_l)) + s_r * (0.5 + h_r * (s_r * s_r))
        gap = y * s_l + ((y + dp) * s_r - du)
        y = jnp.maximum(y - gap * inverse(slope), floor_y)
    s_l = lax.rsqrt(a_l * y + cc_l)
    s_r = lax.rsqrt(a_r * y + e_r)
    pstar = y + p_l
    ustar = 0.5 * ((un_l + un_r) + ((y + dp) * s_r - y * s_l))
    from_left = ustar >= 0.0
    rho = jnp.where(from_left, rho_l, rho_r)
    un = jnp.where(from_left, un_l, un_r)
    ut = jnp.where(from_left, ut_l, ut_r)
    p = jnp.where(from_left, p_l, p_r)
    u_r = ratio * ustar
    mass = u_r * rho
    normal = mass * ustar + ratio * pstar
    trans = mass * ut
    energy = u_r * (2.5 * p + pstar) + (0.5 * mass) * (un * un + ut * ut)
    return mass, normal, trans, energy


def updated(cells, change):
    rho, un, ut, p = cells
    mass, normal, trans, lost = change
    mn = rho * un
    mt = rho * ut
    energy = 2.5 * p + 0.5 * (mn * un + mt * ut)
    rho = rho - mass
    mn = mn - normal
    mt = mt - trans
    energy = energy - lost
    inv = inverse(rho)
    un = mn * inv
    ut = mt * inv
    return rho, un, ut, 0.4 * energy - 0.2 * (mn * un + mt * ut)


def turn_in(source, turned):
    for f in range(4):
        for side in range(SIDES):
            across = source(f, side).T
            for piece in range(PIECES):
                for k in range(LINE // ROWS):
                    at = piece * LINE + k * ROWS
                    turned[f, pl.ds((HALO + k * ROWS) * ROWS + side * PIECES + piece, ROWS, stride=ROWS)] = across[at : at + ROWS]
    shape = (ROWS, LANES)
    row = lax.broadcasted_iota(jnp.int32, shape, 0)
    piece = row & (PIECES - 1)
    lane = lax.broadcasted_iota(jnp.int32, shape, 1)
    for f in range(4):
        for k in range(HALO):
            v = turned[f, pl.ds((LINE + k) * ROWS, ROWS)]
            w = pltpu.roll(v, ROWS, 1)
            seam = jnp.where(lane < ROWS, pltpu.roll(w, 1, 0), pltpu.roll(w, 5, 0))
            turned[f, pl.ds(k * ROWS, ROWS)] = jnp.where(piece == 0, seam, pltpu.roll(v, 1, 0))
            v = turned[f, pl.ds((HALO + k) * ROWS, ROWS)]
            w = pltpu.roll(v, LANES - ROWS, 1)
            seam = jnp.where(lane >= LANES - ROWS, pltpu.roll(w, 7, 0), pltpu.roll(w, 3, 0))
            turned[f, pl.ds((HALO + LINE + k) * ROWS, ROWS)] = jnp.where(piece == PIECES - 1, seam, pltpu.roll(v, 7, 0))


def turn_half(source, beyond, turned):
    edge = jnp.concatenate([rows for f in range(4) for rows in beyond(f)] * 2, axis=0).T
    row = lax.broadcasted_iota(jnp.int32, (ROWS, LANES), 0)
    lane = lax.broadcasted_iota(jnp.int32, (ROWS, LANES), 1)
    pieces = LANES // HALF_LINE
    for f in range(4):
        across = source(f).T
        for piece in range(pieces):
            for k in range(HALF_LINE // ROWS):
                at = piece * HALF_LINE + k * ROWS
                turned[f, pl.ds((HALO + k * ROWS) * ROWS + piece, ROWS, stride=ROWS)] = across[at : at + ROWS]
        before = pltpu.roll(edge[LANES - ROWS :], (LANES - 2 * ROWS * f) % LANES, 1)
        before = jnp.where(lane < ROWS, before, pltpu.roll(across[LANES - ROWS :], ROWS, 1))
        after = pltpu.roll(edge[:ROWS], LANES - 2 * ROWS * (f + 1), 1)
        after = jnp.where(lane >= LANES - ROWS, after, pltpu.roll(across[:ROWS], LANES - ROWS, 1))
        for k in range(HALO):
            v = turned[f, pl.ds((HALF_LINE + k) * ROWS, ROWS)]
            first = jnp.broadcast_to(before[ROWS - HALO + k : ROWS - HALO + k + 1], (ROWS, LANES))
            turned[f, pl.ds(k * ROWS, ROWS)] = jnp.where(row == 0, first, pltpu.roll(v, 1, 0))
            v = turned[f, pl.ds((HALO + k) * ROWS, ROWS)]
            last = jnp.broadcast_to(after[k : k + 1], (ROWS, LANES))
            turned[f, pl.ds((HALO + HALF_LINE + k) * ROWS, ROWS)] = jnp.where(row == ROWS - 1, last, pltpu.roll(v, ROWS - 1, 0))


def turn_out(turned, f, line_columns, first):
    parts = [
        turned[f, pl.ds((1 + k * ROWS) * ROWS + first + piece, ROWS, stride=ROWS)]
        for piece in range(LANES // line_columns)
        for k in range(line_columns // ROWS)
    ]
    return jnp.concatenate(parts, axis=0).T


def turned_sweep(turned, swept, ratio, faces, steps):
    def some(part, last):
        at = pl.multiple_of(part * (faces * ROWS), ROWS)
        cells = [
            turned[f, pl.ds(at, (faces + 5) * ROWS)].reshape(faces + 5, ROWS, LANES) for f in range(4)
        ]
        sides = [edges(c) for c in cells]
        flux = fluxes([s[0] for s in sides], [s[1] for s in sides], ratio)
        change = [now - jnp.concatenate([old, now[:-1]], axis=0) for now, old in zip(flux, last)]
        for f, value in enumerate(updated([c[2:-3] for c in cells], change)):
            swept[f, pl.ds(at, faces * ROWS)] = value.reshape(faces * ROWS, LANES)
        return tuple(now[-1:] for now in flux)

    none = (jnp.zeros((1, ROWS, LANES), jnp.float32),) * 4
    if steps == 1:
        some(0, none)
    else:
        lax.fori_loop(0, steps, some, none)


def column_sweep(source, target, turned, swept, ratio):
    turn_in(source, turned)
    turned_sweep(turned, swept, ratio, FACES, (LINE + 1) // FACES)
    for f in range(4):
        for side in range(SIDES):
            target(f, side, turn_out(swept, f, LINE, side * PIECES))


def half_sweep(ref, block, put, turned, swept, ratio):
    def rows(f, first, n):
        return ref[f, pl.ds(first * ROWS, n * ROWS)]

    blocks = LANES // ROWS
    turn_half(
        lambda f: rows(f, block, blocks),
        lambda f: (rows(f, block - 1, 1), rows(f, block + blocks, 1)),
        turned,
    )
    turned_sweep(turned, swept, ratio, HALF_LINE + 1, 1)
    for f in range(4):
        put(f, turn_out(swept, f, HALF_LINE, 0))


def half(ref, *index):
    return lambda f, side: ref[(f, *index, pl.ds(side * LANES, LANES))]


def into(ref, *index):
    def put(f, side, value):
        ref[(f, *index, pl.ds(side * LANES, LANES))] = value

    return put


def line(quarter, row):
    return pl.ds(quarter * (QUARTER * ROWS) + row, QUARTER, stride=ROWS)


def kernel(
    density, velocity, pressure, done, done_half, left,
    start, first, mid, outer, turned, swept, seam, to_up, to_down, from_up, from_down,
    in_sem, send_sem, recv_sem, ready_sem,
):
    slab = lax.axis_index("slab")
    me = lax.axis_index("pencil")
    count = lax.axis_size("pencil")
    up = lax.rem(me + 1, count)
    down = lax.rem(me + count - 1, count)
    planes = start.shape[1]
    quarters = start.shape[2] // (QUARTER * ROWS)

    place = lax.rem(me, GROUP)
    barrier = pltpu.get_barrier_semaphore()
    pl.semaphore_signal(barrier, inc=1, device_id=(slab, down), device_id_type=MESH)

    @pl.when(place < GROUP - 1)
    def _():
        pl.semaphore_signal(barrier, inc=1, device_id=(slab, up), device_id_type=MESH)

    def load(plane, f):
        source = (density.at[plane], velocity.at[0, plane], velocity.at[1, plane], pressure.at[plane])[f]
        return pltpu.make_async_copy(source, start.at[f, plane], in_sem.at[f, plane])

    def load_all(plane):
        for f in range(4):
            load(plane, f).start()

    load_all(0)

    def copy_up(unit, n):
        part = pl.ds(unit, n)
        return pltpu.make_async_remote_copy(
            to_up.at[part], from_down.at[part], send_sem.at[0, unit], recv_sem.at[0, unit],
            device_id=(slab, up), device_id_type=MESH,
        )

    def copy_down(unit, n):
        part = pl.ds(unit, n)
        return pltpu.make_async_remote_copy(
            to_down.at[part], from_up.at[part], send_sem.at[1, unit], recv_sem.at[1, unit],
            device_id=(slab, down), device_id_type=MESH,
        )

    def last_order(step):
        return (step + quarters - 1) % quarters

    def messages(plane, act):
        @pl.when(plane < planes - 2)
        def _():
            for quarter in range(0, quarters, 2):
                act(plane * quarters + quarter, 2)

        @pl.when(jnp.logical_and(plane >= planes - 2, plane < planes - 1))
        def _():
            for quarter in range(quarters):
                act(plane * quarters + quarter, 1)

        @pl.when(plane == planes - 1)
        def _():
            for step in range(quarters):
                act(plane * quarters + last_order(step), 1)

    def pack(ref, plane, begin=0, end=quarters):
        for quarter in range(begin, end):
            unit = plane * quarters + quarter
            for f in range(4):
                for row in range(HALO):
                    to_up[unit, f * HALO + row] = ref[f, plane, line(quarter, ROWS - HALO + row)]
                    to_down[unit, f * HALO + row] = ref[f, plane, line(quarter, row)]

    def send(copy, plane):
        messages(plane, lambda unit, n: copy(unit, n).start())

    for f in range(4):
        load(0, f).wait()
    pack(start, 0, 0, 2)

    @pl.when(place == 0)
    def _():
        pl.semaphore_wait(barrier, 1)

    @pl.when(place > 0)
    def _():
        pl.semaphore_wait(barrier, 2)

    @pl.when(place == GROUP - 1)
    def _():
        pl.semaphore_signal(ready_sem, inc=1, device_id=(slab, up), device_id_type=MESH)

    ahead = place == GROUP - 1
    for unit in range(0, quarters, 2):
        if unit:
            pack(start, 0, unit, unit + 2)

        @pl.when(ahead)
        def _():
            copy_down(unit, 2).start()

        copy_up(unit, 2).start()

        @pl.when(jnp.logical_and(place > 0, jnp.logical_not(ahead)))
        def _():
            copy_down(unit, 2).start()

    for plane in range(1, planes):
        load_all(plane)

    def first_sweep(step, carry):
        plane = jnp.where(step < 2, 1 - step, step)

        @pl.when(plane > 0)
        def _():
            for f in range(4):
                load(plane, f).wait()

        column_sweep(half(start, plane), into(first, plane), turned, swept, 0.025)

        @pl.when(plane > 0)
        def _():
            pack(first, plane)

        def both(unit, n):
            copy_up(unit, n).start()
            copy_down(unit, n).start()

        held = jnp.logical_and(place == GROUP - 1, plane >= 2)

        @pl.when(jnp.logical_and(jnp.logical_and(plane > 0, place > 0), jnp.logical_not(held)))
        def _():
            messages(plane, both)

        @pl.when(held)
        def _():
            send(copy_down, plane)

        @pl.when(jnp.logical_and(plane > 0, place == 0))
        def _():
            send(copy_up, plane)

        @pl.when(jnp.logical_and(plane == 2, place == 0))
        def _():
            pl.semaphore_wait(ready_sem, 1)
            send(copy_down, 0)
            send(copy_down, 1)

        @pl.when(jnp.logical_and(plane == 3, place == 0))
        def _():
            send(copy_down, 2)
            send(copy_down, 3)

        return carry

    lax.fori_loop(0, planes, first_sweep, 0)

    def arrive(unit, n):
        copy_up(unit, n).wait_recv()
        copy_down(unit, n).wait_recv()

    def outer_sweep():
        messages(0, arrive)
        for quarter in range(quarters):
            for f in range(4):
                for row in range(HALO):
                    outer[f, line(quarter, row)] = from_down[quarter, f * HALO + row]
                    outer[f, line(quarter, HALO + row)] = from_up[quarter, f * HALO + row]
                for row in range(2 * HALO, ROWS):
                    outer[f, line(quarter, row)] = from_down[quarter, f * HALO]
        column_sweep(half(outer), into(outer), turned, swept, 0.025)
        for quarter in range(quarters):
            for f in range(4):
                for row in range(HALO):
                    from_down[quarter, f * HALO + row] = outer[f, line(quarter, row)]
                    from_up[quarter, f * HALO + row] = outer[f, line(quarter, HALO + row)]

    low = ROWS - HALO

    def own_rows(f, plane, quarter, begin, end):
        return [first[f, plane, line(quarter, row)][None] for row in range(begin, end)]

    def finish_rows(cells, change, ref, place, begin):
        for f, value in zip((0, 2, 1, 3), updated(cells, change)):
            for row in range(value.shape[0]):
                ref[f, line(place, begin + row)] = value[row]

    def low_rows(plane, quarter, ref, place):
        unit = plane * quarters + quarter
        sides, cells = [], []
        for f in (0, 2, 1, 3):
            own = own_rows(f, plane, quarter, 0, ROWS)
            sides.append(edges(jnp.concatenate([from_down[unit, pl.ds(f * HALO, HALO)], *own], axis=0)))
            cells.append(jnp.concatenate(own[:low], axis=0))
        flux = fluxes([s[0] for s in sides], [s[1] for s in sides], 0.05)
        finish_rows(cells, [now[1:] - now[:-1] for now in flux], ref, place, 0)
        for f, now in enumerate(flux):
            seam[place, f] = now[low]

    def high_rows(plane, quarter, ref, place):
        unit = plane * quarters + quarter
        sides, cells = [], []
        for f in (0, 2, 1, 3):
            own = own_rows(f, plane, quarter, HALO, ROWS)
            sides.append(edges(jnp.concatenate([*own, from_up[unit, pl.ds(f * HALO, HALO)]], axis=0)))
            cells.append(jnp.concatenate(own[low - HALO :], axis=0))
        flux = fluxes([s[0] for s in sides], [s[1] for s in sides], 0.05)
        change = [now - jnp.concatenate([seam[place, f][None], now[:-1]], axis=0) for f, now in enumerate(flux)]
        finish_rows(cells, change, ref, place, low)

    def later(plane, carry):
        pl.when(plane == 0)(outer_sweep)

        def rows_of(part, copy):
            def one(quarter, inner):
                @pl.when(jnp.logical_and(jnp.logical_and(plane > 0, plane < planes - 2), lax.rem(quarter, 2) == 0))
                def _():
                    copy(plane * quarters + quarter, 2).wait_recv()

                @pl.when(plane >= planes - 2)
                def _():
                    copy(plane * quarters + quarter, 1).wait_recv()

                part(plane, quarter, mid, quarter)
                return inner

            lax.fori_loop(0, quarters, one, 0)

        rows_of(low_rows, copy_up)
        rows_of(high_rows, copy_down)
        column_sweep(half(mid), into(done, plane), turned, swept, 0.025)

        @pl.when(jnp.logical_and(place == GROUP - 1, plane < planes - 2))
        def _():
            send(copy_up, plane + 2)

        return carry

    last = planes - 1
    lax.fori_loop(0, last, later, 0)

    def put(f, value):
        done_half[f] = value

    def last_low(step, carry):
        quarter = last_order(step)
        copy_up(last * quarters + quarter, 1).wait_recv()
        low_rows(last, quarter, left, step)
        return carry

    def last_high(step, carry):
        quarter = last_order(step)
        copy_down(last * quarters + quarter, 1).wait_recv()
        high_rows(last, quarter, left, step)
        return carry

    lax.fori_loop(0, quarters - 1, last_low, 0)
    lax.fori_loop(0, quarters - 1, last_high, 0)
    for f in range(4):
        left[f, pl.ds(quarters * QUARTER * ROWS, QUARTER * ROWS)] = left[f, pl.ds(0, QUARTER * ROWS)]
    last_low(quarters - 1, 0)
    half_sweep(left, LEAD, put, turned, swept, 0.025)
    last_high(quarters - 1, 0)

    def sent(unit, n):
        copy_up(unit, n).wait_send()
        copy_down(unit, n).wait_send()

    for plane in range(planes):
        messages(plane, sent)


def last_kernel(done, done_half, left, new_density, new_velocity, new_pressure, final, turned, swept, out_sem, half_sem):
    planes = done.shape[1]
    total = done.shape[2]
    size = final.shape[1]

    def target(plane, f, first, n):
        part = pl.ds(first, n)
        return (
            new_density.at[plane, part], new_velocity.at[0, plane, part],
            new_velocity.at[1, plane, part], new_pressure.at[plane, part],
        )[f]

    def store(f):
        return pltpu.make_async_copy(done.at[f], target(pl.ds(0, planes), f, 0, total), out_sem.at[f])

    wrap = LEAD * ROWS

    def store_half(f, part):
        source, first, n = (
            (done_half.at[f, pl.ds(0, wrap)], total - wrap, wrap),
            (done_half.at[f, pl.ds(wrap, size - wrap)], 0, size - wrap),
            (final.at[f], size - wrap, size),
        )[part]
        return pltpu.make_async_copy(source, target(planes, f, first, n), half_sem.at[f, part])

    for f in range(4):
        store(f).start()
        store_half(f, 0).start()
        store_half(f, 1).start()

    def put(f, value):
        final[f] = value
        store_half(f, 2).start()

    half_sweep(left, LEAD + LANES // ROWS, put, turned, swept, 0.025)
    for f in range(4):
        store(f).wait()
        for part in range(3):
            store_half(f, part).wait()


def on_device(density, velocity, pressure):
    planes, rows, columns = density.shape
    blocks = columns // LANES
    units = planes * blocks // QUARTER

    def blocked(a):
        lead = a.shape[:-2]
        a = jnp.swapaxes(a.reshape(*lead, rows, blocks, LANES), -3, -2).reshape(*lead, blocks * rows, LANES)
        return pltpu.with_memory_space_constraint(a, pltpu.HBM)

    def unblocked(a):
        lead = a.shape[:-2]
        return jnp.swapaxes(a.reshape(*lead, blocks, rows, LANES), -3, -2).reshape(*lead, rows, columns)

    hbm = pl.BlockSpec(memory_space=pltpu.HBM)
    vmem = pl.BlockSpec(memory_space=pltpu.VMEM)
    plane = (blocks * rows, LANES)
    f32 = jnp.float32
    halo = (units, 4 * HALO, QUARTER, LANES)
    half_plane = (4, LANES, LANES)
    work = [
        pltpu.VMEM((4, (LINE + 2 * HALO) * ROWS, LANES), f32),
        pltpu.VMEM((4, (LINE + 1) * ROWS, LANES), f32),
    ]
    middle = pl.pallas_call(
        kernel,
        out_shape=(
            pltpu.VMEM((4, planes - 1, *plane), f32),
            pltpu.VMEM(half_plane, f32),
            pltpu.VMEM((4, (blocks + QUARTER) * rows, LANES), f32),
        ),
        in_specs=[hbm] * 3,
        out_specs=(vmem,) * 3,
        scratch_shapes=[
            pltpu.VMEM((4, planes, *plane), f32),
            pltpu.VMEM((4, planes, *plane), f32),
            pltpu.VMEM((4, *plane), f32),
            pltpu.VMEM((4, *plane), f32),
            *work,
            pltpu.VMEM((blocks // QUARTER, 4, QUARTER, LANES), f32),
            pltpu.VMEM(halo, f32),
            pltpu.VMEM(halo, f32),
            pltpu.VMEM(halo, f32),
            pltpu.VMEM(halo, f32),
            pltpu.SemaphoreType.DMA((4, planes)),
            pltpu.SemaphoreType.DMA((2, units)),
            pltpu.SemaphoreType.DMA((2, units)),
            pltpu.SemaphoreType.REGULAR,
        ],
        compiler_params=pltpu.CompilerParams(
            collective_id=0, has_side_effects=True, vmem_limit_bytes=32 * 2**20
        ),
    )(blocked(density), blocked(velocity), blocked(pressure))
    outs = pl.pallas_call(
        last_kernel,
        out_shape=(pltpu.HBM((planes, *plane), f32), pltpu.HBM((2, planes, *plane), f32), pltpu.HBM((planes, *plane), f32)),
        in_specs=[vmem] * 3,
        out_specs=(hbm,) * 3,
        scratch_shapes=[
            pltpu.VMEM(half_plane, f32),
            *work,
            pltpu.SemaphoreType.DMA((4,)),
            pltpu.SemaphoreType.DMA((4, 3)),
        ],
        compiler_params=pltpu.CompilerParams(vmem_limit_bytes=16 * 2**20),
    )(*(pltpu.with_memory_space_constraint(a, pltpu.VMEM) for a in middle))
    return tuple(unblocked(a) for a in outs)


def solution(mesh):
    one = P("slab", "pencil", None)
    two = P(None, "slab", "pencil", None)
    return jax.shard_map(on_device, mesh=mesh, in_specs=(one, two, one), out_specs=(one, two, one), check_vma=False)
```
